128 devices in a mesh: lat: 32 (over x, z, core), lev: 4 (over y).
Axes of the slice: x: 4, y: 4, z: 4, core: 2. Of those that a mesh axis runs over, the one named last changes fastest.
Arguments:
- fields: float32 [4, 256, 128, 1024], P(None, 'lat', 'lev'), may hold values from -6 to 6
- thickness: float32 [256, 128, 1024], P('lat', 'lev'), may hold values from 0.5 to 1.5
- courant_lon: float32 [256, 128, 1024], P('lat', 'lev'), may hold values from -0.8 to 0.8
- courant_lat: float32 [256, 128, 1024], P('lat', 'lev'), may hold values from -0.8 to 0.8
- exchange: float32 [2, 128, 128], replicated, may hold values from -0.5 to 0.5
- solar_profile: float32 [128], replicated, may hold values from 0.1 to 1
- owners: int32 [2048, 1], P(('lat', 'lev')), may hold values from 0 to 31; in each aligned block of 16 rows (0 to 15, 16 to 31, ...) at most 2 rows name the same one
- daylight: int32 [2048], P(('lat', 'lev')), may hold values 0 or 1
Outputs:
- remapped: float32 [4, 256, 128, 1024], P(None, 'lat', None, 'lev')
- heating: float32 [256, 128, 1024], P('lat', None, 'lev')
- owner_heat: float32 [32, 4], P('lat', 'lev')
The draws below stay inside these ranges and needn't reach their ends.
Inputs may be any that keep to these rules, and one draw needn't show every extreme that they name: `owners`: among the rows of one device at most 2 name the same owner.
All inputs are finite; a program needn't handle non-finite values. No bound on the sum of `daylight` on one device may be relied on, other than what follows from the above.
Results may differ from the reference program's by a relative error of at most 0.0003.
Values sent between devices are 32-bit elements; how exact they have to be, the bound alone decides.
No kernel may reach another device: no remote copies, remote signals or barrier semaphores. Data moves between devices by JAX's collectives and lax.ppermute only.
A program may use at most 128 MiB of HBM per device.

```python
import math
import jax
import jax.numpy as jnp
import numpy as np
from jax import lax

NLON = 1024
NLEV = 128
FIELDS = 4
BANDS = 2
BLOCK_COLS = 128
CAP = 2
LAT_DEV = 8
NLAT = 256
PIECE = 256
NB = 16
BLOCKS = 2048
OWNERS = 32
N_LAT = 32
N_LEV = 4


def place_ends(drawn, rng, low, high):
    longest = drawn.shape.index(max(drawn.shape))
    spots = []
    for shift in (0, 1):
        where = [jax.random.randint(jax.random.fold_in(rng, axis), (), 0, length) for axis, length in enumerate(drawn.shape)]
        where[longest] = (where[longest] + shift) % drawn.shape[longest]
        spots.append(tuple(where))
    return drawn.at[spots[0]].set(low).at[spots[1]].set(high)


def shard_levels(own_key, dims, split, smallest, largest):
    def one(axis_at, blocks):
        steps = jax.random.uniform(jax.random.fold_in(jax.random.fold_in(own_key, 6), axis_at), (blocks,), jnp.float32, smallest / len(split), largest / len(split))
        return jnp.repeat(jnp.exp(steps), dims[axis_at] // blocks).reshape((-1,) + (1,) * (len(dims) - axis_at - 1))

    level = one(*split[0])
    for cut in split[1:]:
        level = level * one(*cut)
    return level


def routed_block(key, own, number, rows, number_of, top, limit, skew):
    ranking = jax.random.permutation(key, number_of)
    crowded, usual = portions_of(number_of, rows * top, limit, skew, True), portions_of(number_of, rows * top, limit, skew, False)
    places = jnp.arange(number_of)

    def named(sizes, rotation):
        used = int((sizes > 0).sum())
        fixed = max(1, used // 4)
        passed = fixed + (places - fixed + rotation * (used - fixed)) % max(1, number_of - fixed)
        return jnp.zeros((number_of,), jnp.int32).at[ranking[jnp.where(places < fixed, places, passed)]].set(jnp.asarray(sizes, jnp.int32))

    sizes = jnp.where(number % 4 == 0, named(crowded, number // 4), named(usual, number - number // 4 - 1))
    mixed = jax.random.permutation(jax.random.fold_in(own, 3), number_of)
    source_of, taker = mixed[0:number_of // 2 * 2:2], mixed[1:number_of // 2 * 2:2]
    margin = jnp.minimum(sizes[source_of] - 1, limit - sizes[taker]) // 2
    margin = jnp.where((source_of == ranking[0]) | (taker == ranking[0]) | (sizes[taker] == 0), 0, jnp.maximum(margin, 0))
    passed = jax.random.randint(jax.random.fold_in(own, 4), (number_of // 2,), 0, 1 << 20) % (margin + 1)
    sizes = sizes.at[source_of].add(-passed).at[taker].add(passed)
    labels = jnp.searchsorted(jnp.cumsum(sizes), jnp.arange(rows * top), side="right").astype(jnp.int32)
    grid = labels.reshape(top, rows).T
    grid = grid[jax.random.permutation(jax.random.fold_in(own, 1), rows)]
    rotation = jax.random.randint(jax.random.fold_in(own, 2), (rows, 1), 0, top)
    return jnp.take_along_axis(grid, (jnp.arange(top)[None, :] + rotation) % top, axis=1)


def portions_of(amount, total, bound, lean, full):
    portions = [(1 << 20) // math.isqrt(grade ** lean) + 1 for grade in range(1, amount + 1)]
    largest = bound if full else min(bound, max(-(-total // amount), total * portions[0] // sum(portions)))
    least = 1 if total - largest >= amount - 1 else 0
    counts, surplus = [largest] + [least] * (amount - 1), total - largest - least * (amount - 1)
    while surplus > 0:
        free = [i for i in range(1, amount) if counts[i] < largest] or [i for i in range(1, amount) if counts[i] < bound]
        mass, left = sum([portions[i] for i in free]), surplus
        for i in free:
            extra = min(bound - counts[i], max(1, left * portions[i] // mass), surplus)
            counts[i] = counts[i] + extra
            surplus = surplus - extra
    return np.array(counts)


def noise(own_key, extent, deviation, limit, shards=(), kind=jnp.bfloat16):
    array = jax.random.normal(own_key, extent, jnp.float32) * deviation
    if len(shards) > 0:
        array = shard_levels(own_key, extent, shards, -0.22, 0.18) * array
    return jnp.clip(array, min=-limit, max=limit).astype(kind)


def setup_inputs(seed: int = 0) -> dict:
    streams_of = jax.random.split(jax.random.key(seed), 9)
    fields = noise(streams_of[0], (FIELDS, NLAT, NLEV, NLON), 1.0, 6.0, ((1, 32), (2, 4)), jnp.float32)
    thickness = jnp.clip(0.5 + 1.0 * jax.random.uniform(streams_of[1], (NLAT, NLEV, NLON), jnp.float32) ** shard_levels(streams_of[1], (NLAT, NLEV, NLON), ((0, 32), (1, 4)), -0.2, 0.2), 0.5, 1.5)
    courant_lon = jnp.clip(jax.random.uniform(streams_of[2], (NLAT, NLEV, NLON), jnp.float32, -0.8, 0.8) * shard_levels(streams_of[2], (NLAT, NLEV, NLON), ((0, 32), (1, 4)), -0.4, 0.0), -0.8, 0.8)
    courant_lat = jnp.clip(jax.random.uniform(streams_of[3], (NLAT, NLEV, NLON), jnp.float32, -0.8, 0.8) * shard_levels(streams_of[3], (NLAT, NLEV, NLON), ((0, 32), (1, 4)), -0.4, 0.0), -0.8, 0.8)
    exchange = noise(streams_of[4], (BANDS, NLEV, NLEV), NLEV ** -0.5, 0.5, (), jnp.float32)
    solar_profile = jnp.clip(jnp.exp(jax.random.uniform(streams_of[5], (NLEV,), jnp.float32, math.log(0.1), math.log(1.0))), 0.1, 1.0)
    owners_keys = jax.random.split(jax.random.fold_in(streams_of[6], 1), BLOCKS // NB)
    owners_turns = jax.random.permutation(jax.random.fold_in(streams_of[6], 3), BLOCKS // NB)
    owners = jax.vmap(lambda own, number: routed_block(jax.random.fold_in(streams_of[6], 2), own, number, NB, OWNERS, 1, CAP, 2))(owners_keys, owners_turns).reshape((BLOCKS, 1))
    daylight = place_ends((jax.random.randint(streams_of[7], (BLOCKS,), 0, 2) < 1).astype(jnp.int32), jax.random.fold_in(streams_of[7], 1), 0, 1)
    return dict(fields=fields, thickness=thickness, courant_lon=courant_lon, courant_lat=courant_lat, exchange=exchange, solar_profile=solar_profile, owners=owners, daylight=daylight)


HIGH = lax.Precision.HIGHEST


def wendroff(values, courant, plus, minus):
    return values - 0.5 * courant * (plus - minus) + 0.5 * courant * courant * (plus - 2.0 * values + minus)


def remap_row(row_fields, row_thick):
    levels = row_thick.shape[0]
    index = jnp.arange(levels)
    lower = (index[:, None] >= index[None, :]).astype(jnp.float32)
    upper_edge = jnp.dot(lower, row_thick, precision=HIGH, preferred_element_type=jnp.float32)
    lower_edge = upper_edge - row_thick
    spacing = upper_edge[-1] / levels
    steps_f = index.astype(jnp.float32)
    ref_lo = steps_f[:, None] * spacing[None, :]
    ref_hi = (steps_f + 1.0)[:, None] * spacing[None, :]
    intersection = jnp.maximum(jnp.minimum(ref_hi[:, None, :], upper_edge[None, :, :]) - jnp.maximum(ref_lo[:, None, :], lower_edge[None, :, :]), 0.0)
    mixed = jnp.einsum('ijc,fjc->fic', intersection, row_fields, precision=HIGH)
    return mixed / spacing[None, None, :]


def physics(temp, humid, day, exchange, solar, form):
    square = humid * humid
    absorb = square / (1.0 + square)
    clear = 1.0 / (1.0 + square)
    heat = jnp.einsum(form, exchange[0], absorb * temp, precision=HIGH)
    heat = heat + jnp.einsum(form, exchange[1], clear * temp, precision=HIGH)
    return heat + day * solar * clear


def reference(fields, thickness, courant_lon, courant_lat, exchange, solar_profile, owners, daylight):
    plus = jnp.roll(fields, -1, axis=3)
    minus = jnp.roll(fields, 1, axis=3)
    stepped = wendroff(fields, courant_lon[None], plus, minus)
    padded = jnp.pad(stepped, ((0, 0), (1, 1), (0, 0), (0, 0)))
    stepped = wendroff(stepped, courant_lat[None], padded[:, 2:], padded[:, :-2])

    def one_row(row):
        row_fields = lax.dynamic_index_in_dim(stepped, row, 1, keepdims=False)
        row_thick = lax.dynamic_index_in_dim(thickness, row, 0, keepdims=False)
        return remap_row(row_fields, row_thick)

    remapped = jnp.moveaxis(lax.map(one_row, jnp.arange(NLAT)), 0, 1)
    per_row = PIECE // BLOCK_COLS
    day_grid = daylight.reshape(N_LAT, N_LEV, LAT_DEV, per_row).transpose(0, 2, 1, 3).reshape(NLAT, N_LEV * per_row)
    day_cols = jnp.repeat(day_grid.astype(jnp.float32), BLOCK_COLS, axis=1)
    heat = physics(remapped[0], remapped[1], day_cols[:, None, :], exchange, solar_profile[:, None], 'ij,ajc->aic')
    means = jnp.sum(heat.reshape(NLAT, NLEV, N_LEV * per_row, BLOCK_COLS), axis=(1, 3)) / (NLEV * BLOCK_COLS)
    means = means.reshape(N_LAT, LAT_DEV, N_LEV, per_row).transpose(0, 2, 1, 3).reshape(N_LAT, N_LEV, NB)
    onehot = (owners[:, 0].reshape(N_LAT, N_LEV, NB)[..., None] == jnp.arange(OWNERS)[None, None, None, :]).astype(jnp.float32)
    owner_heat = jnp.sum(onehot * means[..., None], axis=(0, 2)).T
    return (remapped, heat, owner_heat)
```

```python
import jax
import jax.numpy as jnp
from jax import lax
from jax.experimental import pallas as pl
from jax.experimental.pallas import tpu as pltpu
from jax.sharding import PartitionSpec as P

F32 = jnp.float32
HIGH = lax.Precision.HIGHEST
ANY = pl.BlockSpec(memory_space=pl.ANY)
SMEM = pl.BlockSpec(memory_space=pltpu.SMEM)
BLOCK = 128
STEP = 8
VMEM_LIMIT = 48 * 1024 * 1024


def cost(flops, nbytes):
    return pl.CostEstimate(flops=flops, bytes_accessed=nbytes, transcendentals=0)


def params():
    return pltpu.CompilerParams(vmem_limit_bytes=VMEM_LIMIT)


def coefs(c):
    sq = 0.5 * c * c
    half = 0.5 * c
    return 1.0 - 2.0 * sq, sq - half, sq + half


def lon_step(x, w):
    n = x.shape[-1]
    mid, up, down = w
    return mid * x + up * pltpu.roll(x, n - 1, 1) + down * pltpu.roll(x, 1, 1)


def prep_kernel(head_in, tail_in, c_head, c_tail, thick, head, tail, t1, t2, t3, sems):
    step = pl.program_id(0)
    me = lax.axis_index("lev")
    width = t1.shape[-1]

    def copies():
        out = []
        for s, dst in enumerate((t1, t2, t3)):
            at = pl.multiple_of(lax.rem(me + s + 1, 4) * width, width)
            out.append(pltpu.make_async_copy(thick.at[:, :, pl.ds(at, width)], dst, sems.at[s]))
        return out

    @pl.when(step == 0)
    def _():
        for c in copies():
            c.start()

    for src, cour, dst in ((head_in, c_head, head), (tail_in, c_tail, tail)):
        w = coefs(cour[0])
        for f in range(src.shape[0]):
            dst[f] = lon_step(src[f, 0], w)

    @pl.when(step == pl.num_programs(0) - 1)
    def _():
        for c in copies():
            c.wait()


def prep(fields, courant_lon, thickness):
    nf, rows, levs, lon = fields.shape
    width = lon // 4
    edge = lambda r: pl.BlockSpec((nf, 1, 8, lon), lambda i: (0, r, i, 0))
    cedge = lambda r: pl.BlockSpec((1, 8, lon), lambda i: (r, i, 0))
    out_edge = pl.BlockSpec((nf, 8, lon), lambda i: (0, i, 0))
    piece = jax.ShapeDtypeStruct((rows, levs, width), F32)
    side = jax.ShapeDtypeStruct((nf, levs, lon), F32)
    return pl.pallas_call(
        prep_kernel,
        grid=(levs // 8,),
        in_specs=[edge(0), edge(rows - 1), cedge(0), cedge(rows - 1), ANY],
        out_specs=[out_edge, out_edge, ANY, ANY, ANY],
        out_shape=[side, side, piece, piece, piece],
        scratch_shapes=[pltpu.SemaphoreType.DMA((3,))],
        compiler_params=params(),
        cost_estimate=cost(10 * 2 * nf * levs * lon, 6 * 1024 * 1024),
        name="prep",
    )(fields, fields, courant_lon, courant_lon, thickness)


def advect_kernel(q, c_lon, c_lat, prev, nxt, o0, o1, o2, o3, keep, sems):
    step = pl.program_id(0)
    last = pl.num_programs(0) - 1
    me = lax.axis_index("lev")
    width = o0.shape[-1]
    nf, rows = q.shape[0], q.shape[1]

    def copies(k):
        out = []
        for s, dst in enumerate((o0, o1, o2, o3)):
            at = pl.multiple_of(lax.rem(me + s, 4) * width, width)
            lev = pl.multiple_of(k * 8, 8)
            out.append(
                pltpu.make_async_copy(
                    keep.at[k, :, :, :, pl.ds(at, width)], dst.at[:, :, pl.ds(lev, 8), :], sems.at[k, s]
                )
            )
        return out

    before = [prev[f] for f in range(nf)]
    w = coefs(c_lon[0])
    here = [lon_step(q[f, 0], w) for f in range(nf)]
    for r in range(rows):
        if r + 1 < rows:
            w = coefs(c_lon[r + 1])
            after = [lon_step(q[f, r + 1], w) for f in range(nf)]
        else:
            after = [nxt[f] for f in range(nf)]
        mid, up, down = coefs(c_lat[r])
        for f in range(nf):
            keep[step, f, r] = mid * here[f] + up * after[f] + down * before[f]
        before, here = here, after
    for c in copies(step):
        c.start()

    @pl.when(step == last)
    def _():
        for k in range(4):
            for c in copies(k):
                c.wait()


def advect(group, fields, c_lon, c_lat, prev, nxt):
    nf, rows, levs, lon = fields.shape
    half = nf // 2
    width = lon // 4
    steps = levs // 8
    cspec = pl.BlockSpec((rows, 8, lon), lambda i: (0, i, 0))
    hspec = pl.BlockSpec((half, 8, lon), lambda i: (group, i, 0))
    piece = jax.ShapeDtypeStruct((half, rows, levs, width), F32)
    return pl.pallas_call(
        advect_kernel,
        grid=(steps,),
        in_specs=[pl.BlockSpec((half, rows, 8, lon), lambda i: (group, 0, i, 0)), cspec, cspec, hspec, hspec],
        out_specs=[ANY] * 4,
        out_shape=[piece] * 4,
        scratch_shapes=[pltpu.VMEM((steps, half, rows, 8, lon), F32), pltpu.SemaphoreType.DMA((steps, 4))],
        compiler_params=params(),
        cost_estimate=cost(25 * half * rows * levs * lon, 7 * 1024 * 1024),
        name="advect",
    )(fields, c_lon, c_lat, prev, nxt)


def edges_kernel(own, r1, r2, r3, e_ref, lo_ref, n_ref, col):
    r = pl.program_id(0)
    me = lax.axis_index("lev")
    quarter = own.shape[1]
    levels = 4 * quarter
    for s, src in enumerate((own, r1, r2, r3)):
        at = pl.multiple_of(lax.rem(me + 4 - s, 4) * quarter, quarter)
        col[pl.ds(at, quarter), :] = src[0]
    i = lax.broadcasted_iota(jnp.int32, (levels, levels), 0)
    j = lax.broadcasted_iota(jnp.int32, (levels, levels), 1)
    lower = (i >= j).astype(F32)
    upper = jnp.dot(lower, col[...], precision=HIGH, preferred_element_type=F32)
    e = upper * (levels / upper[levels - 1 :, :])
    e_ref[0] = e
    first = jnp.min(e, axis=1, keepdims=True)
    final = jnp.max(e, axis=1, keepdims=True)
    start = (lax.broadcasted_iota(jnp.int32, (levels, BLOCK), 1) * 8).astype(F32)
    lo = jnp.sum((final <= start).astype(F32), axis=0, keepdims=True)
    hi = jnp.sum((first < start + 8.0).astype(F32), axis=0, keepdims=True)
    lo = jnp.minimum(lo, levels - 1.0).astype(jnp.int32)
    hi = jnp.minimum(hi, levels - 1.0).astype(jnp.int32)
    n = lax.shift_right_logical(hi - lo + STEP, 3)
    lo_ref[0] = jnp.maximum(jnp.minimum(lo, levels - STEP * n), 0)
    n_ref[0] = n


def edges(own, r1, r2, r3):
    rows, quarter, _ = own.shape
    width = r1.shape[-1]
    levels = 4 * quarter
    mine = lax.dynamic_slice_in_dim(own, lax.axis_index("lev") * width, width, 2)
    spec = pl.BlockSpec((1, quarter, width), lambda r: (r, 0, 0))
    bound = jax.ShapeDtypeStruct((rows, 1, BLOCK), jnp.int32)
    bspec = pl.BlockSpec((1, 1, BLOCK), lambda r: (r, 0, 0))
    return pl.pallas_call(
        edges_kernel,
        grid=(rows,),
        in_specs=[spec] * 4,
        out_specs=[pl.BlockSpec((1, levels, width), lambda r: (r, 0, 0)), bspec, bspec],
        out_shape=[jax.ShapeDtypeStruct((rows, levels, width), F32), bound, bound],
        scratch_shapes=[pltpu.VMEM((levels, width), F32)],
        compiler_params=params(),
        cost_estimate=cost(12 * rows * levels * levels * width, 2 * 1024 * 1024),
        name="edges",
    )(mine, r1, r2, r3)


def remap_row(r, lo_ref, n_ref, e_ref, pieces, cols, out):
    me = lax.axis_index("lev")
    nf = cols.shape[0]
    width = cols.shape[2]
    quarter = pieces[0].shape[2]
    for s, src in enumerate(pieces):
        at = pl.multiple_of(lax.rem(me + 4 - s, 4) * quarter, quarter)
        for f in range(nf):
            cols[f, pl.ds(at, quarter), :] = src[f, 0]
    level = lax.broadcasted_iota(jnp.int32, (8, width), 0)
    groups = 4 * quarter // 8

    def group(g, _):
        index = (level + g * 8).astype(F32)
        lo = lo_ref[r, 0, g]

        def some(k, carry):
            old = carry[0]
            accs = list(carry[1:])
            j0 = lo + k * STEP
            for t in range(STEP):
                u = jnp.minimum(jnp.maximum(e_ref[0, pl.ds(j0 + t, 1), :] - index, 0.0), 1.0)
                w = u - old
                old = u
                for f in range(nf):
                    accs[f] = accs[f] + w * cols[f, pl.ds(j0 + t, 1), :]
            return (old, *accs)

        zero = jnp.zeros((8, width), F32)
        res = lax.fori_loop(0, n_ref[r, 0, g], some, (zero,) * (nf + 1))
        at = pl.multiple_of(g * 8, 8)
        for f in range(nf):
            out[f, 0, pl.ds(at, 8), :] = res[1 + f]
        return 0

    lax.fori_loop(0, groups, group, 0)


def heat_kernel(
    lo_ref, n_ref, own_ref, day_ref, e_ref, p0, p1, p2, p3, exch, solar, out, heating, shares, cols
):
    r = pl.program_id(0)
    remap_row(r, lo_ref, n_ref, e_ref, (p0, p1, p2, p3), cols, out)
    temp = out[0, 0]
    hum = out[1, 0]
    levels, width = temp.shape
    square = hum * hum
    clear = 1.0 / (1.0 + square)
    absorb = square * clear
    heat = jnp.dot(exch[0], absorb * temp, precision=HIGH, preferred_element_type=F32)
    heat = heat + jnp.dot(exch[1], clear * temp, precision=HIGH, preferred_element_type=F32)
    lane = lax.broadcasted_iota(jnp.int32, (1, width), 1)
    d0 = jnp.full((1, width), day_ref[2 * r], jnp.int32)
    d1 = jnp.full((1, width), day_ref[2 * r + 1], jnp.int32)
    day = jnp.where(lane < BLOCK, d0, d1).astype(F32)
    heat = heat + (day * solar[...]) * clear
    heating[0] = heat
    total = jnp.sum(heat, axis=0, keepdims=True)
    line = lax.broadcasted_iota(jnp.int32, (1, BLOCK), 1)

    @pl.when(r == 0)
    def _():
        shares[...] = jnp.zeros_like(shares)

    acc = shares[...]
    for b in range(2):
        mean = jnp.sum(total[:, b * BLOCK : (b + 1) * BLOCK], axis=1, keepdims=True) * (1.0 / (levels * BLOCK))
        acc = acc + jnp.where(line == own_ref[2 * r + b], mean, 0.0)
    shares[...] = acc


def remap_kernel(lo_ref, n_ref, e_ref, p0, p1, p2, p3, base, out, cols):
    remap_row(pl.program_id(0), lo_ref, n_ref, e_ref, (p0, p1, p2, p3), cols, out)


def remap(group, lo, n, e, pieces, base=None, heat_args=None):
    half, rows, quarter, width = pieces[0].shape
    levels = 4 * quarter
    espec = pl.BlockSpec((1, levels, width), lambda r: (r, 0, 0))
    pspec = pl.BlockSpec((half, 1, quarter, width), lambda r: (0, r, 0, 0))
    ospec = pl.BlockSpec((half, 1, levels, width), lambda r: (group, r, 0, 0))
    full = jax.ShapeDtypeStruct((2 * half, rows, levels, width), F32)
    common = dict(
        grid=(rows,),
        scratch_shapes=[pltpu.VMEM((half, levels, width), F32)],
        compiler_params=params(),
    )
    if heat_args is None:
        return pl.pallas_call(
            remap_kernel,
            in_specs=[SMEM, SMEM, espec] + [pspec] * 4 + [ANY],
            out_specs=ospec,
            out_shape=full,
            input_output_aliases={7: 0},
            cost_estimate=cost(200 * half * rows * levels * width, 5 * 1024 * 1024),
            name="remap",
            **common,
        )(lo, n, e, *pieces, base)
    owners, day, exchange, solar = heat_args
    hspec = pl.BlockSpec((1, levels, width), lambda r: (r, 0, 0))
    return pl.pallas_call(
        heat_kernel,
        in_specs=[SMEM, SMEM, SMEM, SMEM, espec]
        + [pspec] * 4
        + [pl.BlockSpec((2, levels, levels), lambda r: (0, 0, 0)), pl.BlockSpec((levels, 1), lambda r: (0, 0))],
        out_specs=[ospec, hspec, pl.BlockSpec((1, BLOCK), lambda r: (0, 0))],
        out_shape=[full, jax.ShapeDtypeStruct((rows, levels, width), F32), jax.ShapeDtypeStruct((1, BLOCK), F32)],
        cost_estimate=cost(300 * half * rows * levels * width, 7 * 1024 * 1024),
        name="heat",
        **common,
    )(lo, n, owners, day, e, *pieces, exchange, solar)


def per_device(fields, thickness, courant_lon, courant_lat, exchange, solar_profile, owners, daylight):
    count = lax.axis_size("lat")
    ends = count - 1
    turn = lambda s: [(i, (i + s) % 4) for i in range(4)]
    around = lambda ps: [ps[0]] + [lax.ppermute(p, "lev", turn(s + 1)) for s, p in enumerate(ps[1:])]

    head, tail, t1, t2, t3 = prep(fields, courant_lon, thickness)
    prev = lax.ppermute(tail, "lat", [(i, i + 1) for i in range(ends)])
    nxt = lax.ppermute(head, "lat", [(i + 1, i) for i in range(ends)])
    thick = around([thickness, t1, t2, t3])
    e, lo, n = edges(*thick)
    first = around(advect(0, fields, courant_lon, courant_lat, prev, nxt))
    second = around(advect(1, fields, courant_lon, courant_lat, prev, nxt))
    heat_args = (owners[:, 0], daylight, exchange, solar_profile[:, None])
    remapped, heating, shares = remap(0, lo, n, e, first, heat_args=heat_args)
    remapped = remap(1, lo, n, e, second, base=remapped)
    shares = shares[0, :count].reshape(count, 1, 1)
    owner_heat = jnp.sum(lax.all_to_all(shares, "lat", split_axis=0, concat_axis=0, tiled=True)).reshape(1, 1)
    return (remapped, heating, owner_heat)


def solution(mesh):
    placed = (
        P(None, "lat", "lev", None),
        P("lat", "lev", None),
        P("lat", "lev", None),
        P("lat", "lev", None),
        P(),
        P(),
        P(("lat", "lev"), None),
        P(("lat", "lev")),
    )
    return jax.shard_map(
        per_device,
        mesh=mesh,
        in_specs=placed,
        out_specs=(P(None, "lat", None, "lev"), P("lat", None, "lev"), P("lat", "lev")),
        check_vma=False,
    )
```

```python
import jax
import jax.numpy as jnp
from jax import lax
from jax.experimental import pallas as pl
from jax.experimental.pallas import tpu as pltpu
from jax.sharding import PartitionSpec as P

F32 = jnp.float32
HIGH = lax.Precision.HIGHEST
ANY = pl.BlockSpec(memory_space=pl.ANY)
SMEM = pl.BlockSpec(memory_space=pltpu.SMEM)
BLOCK = 128
PAD = 48
RUN = 4
BUNCH = 4
MIB = 1024 * 1024


COST = pl.CostEstimate(flops=1, bytes_accessed=1, transcendentals=0)


def params(mib):
    return pltpu.CompilerParams(vmem_limit_bytes=mib * MIB)


def coefs(c):
    sq = 0.5 * c * c
    half = 0.5 * c
    return 1.0 - 2.0 * sq, sq - half, sq + half


def lon_step(x, w):
    n = x.shape[-1]
    mid, up, down = w
    return mid * x + up * pltpu.roll(x, n - 1, 1) + down * pltpu.roll(x, 1, 1)


def prep_kernel(head_in, tail_in, c_head, c_tail, thick, head, tail, sent, sems):
    step = pl.program_id(0)

    def copies():
        out = []
        for s in range(4):
            for h in range(2):
                at = (2 * s + h) * BLOCK
                out.append(pltpu.make_async_copy(thick.at[:, :, pl.ds(at, BLOCK)], sent.at[s, :, h], sems.at[s, h]))
        return out

    @pl.when(step == 0)
    def _():
        for c in copies():
            c.start()

    for src, cour, dst in ((head_in, c_head, head), (tail_in, c_tail, tail)):
        w = coefs(cour[0])
        for f in range(src.shape[0]):
            dst[f] = lon_step(src[f, 0], w)

    @pl.when(step == pl.num_programs(0) - 1)
    def _():
        for c in copies():
            c.wait()


def prep(fields, courant_lon, thickness):
    nf, rows, levs, lon = fields.shape
    edge = lambda r: pl.BlockSpec((nf, 1, 8, lon), lambda i: (0, r, i, 0))
    cedge = lambda r: pl.BlockSpec((1, 8, lon), lambda i: (r, i, 0))
    out_edge = pl.BlockSpec((nf, 8, lon), lambda i: (0, i, 0))
    piece = jax.ShapeDtypeStruct((4, rows, 2, levs, BLOCK), F32)
    side = jax.ShapeDtypeStruct((nf, levs, lon), F32)
    return pl.pallas_call(
        prep_kernel,
        grid=(levs // 8,),
        in_specs=[edge(0), edge(rows - 1), cedge(0), cedge(rows - 1), ANY],
        out_specs=[out_edge, out_edge, ANY],
        out_shape=[side, side, piece],
        scratch_shapes=[pltpu.SemaphoreType.DMA((4, 2))],
        compiler_params=params(58),
        cost_estimate=COST,
        name="prep",
    )(fields, fields, courant_lon, courant_lon, thickness)


def advect_kernel(q, c_lon, c_lat, prev, nxt, after, *rest):
    *sent, keep, sems = rest
    step = pl.program_id(0)
    last = pl.num_programs(0) - 1
    nf, rows = q.shape[0], q.shape[1]

    def copies(k):
        out = []
        for s in range(4):
            for h in range(2):
                at, dst = (2 * s + h) * BLOCK, sent[0].at[s] if len(sent) == 1 else sent[s]
                if len(sent) > 1:
                    at = pl.multiple_of(lax.rem(lax.axis_index("lev") + s, 4) * (2 * BLOCK) + h * BLOCK, BLOCK)
                lev = pl.multiple_of(k * 8, 8)
                out.append(
                    pltpu.make_async_copy(
                        keep.at[k, :, :, :, pl.ds(at, BLOCK)], dst.at[:, :, h, pl.ds(lev, 8), :], sems.at[k, s, h]
                    )
                )
        return out

    before = [prev[f] for f in range(nf)]
    w = coefs(c_lon[0])
    here = [lon_step(q[f, 0], w) for f in range(nf)]
    for r in range(rows):
        if r + 1 < rows:
            w = coefs(c_lon[r + 1])
            ahead = [lon_step(q[f, r + 1], w) for f in range(nf)]
        else:
            ahead = [nxt[f] for f in range(nf)]
        mid, up, down = coefs(c_lat[r])
        for f in range(nf):
            keep[step, f, r] = mid * here[f] + up * ahead[f] + down * before[f]
        before, here = here, ahead
    for c in copies(step):
        c.start()

    @pl.when(step == last)
    def _():
        for k in range(4):
            for c in copies(k):
                c.wait()


def advect(group, fields, c_lon, c_lat, prev, nxt, stacked, after):
    nf, rows, levs, lon = fields.shape
    half = nf // 2
    steps = levs // 8
    cspec = pl.BlockSpec((rows, 8, lon), lambda i: (0, i, 0))
    hspec = pl.BlockSpec((half, 8, lon), lambda i: (group, i, 0))
    shape = (half, rows, 2, levs, BLOCK)
    piece = [jax.ShapeDtypeStruct((4, *shape), F32)] if stacked else [jax.ShapeDtypeStruct(shape, F32)] * 4
    return pl.pallas_call(
        advect_kernel,
        grid=(steps,),
        in_specs=[pl.BlockSpec((half, rows, 8, lon), lambda i: (group, 0, i, 0)), cspec, cspec, hspec, hspec, ANY],
        out_specs=[ANY] * len(piece),
        out_shape=piece,
        scratch_shapes=[pltpu.VMEM((steps, half, rows, 8, lon), F32), pltpu.SemaphoreType.DMA((steps, 4, 2))],
        compiler_params=params(58),
        cost_estimate=COST,
        name="advect",
    )(fields, c_lon, c_lat, prev, nxt, after)


def edges_kernel(thick, e_ref, lo_ref, n_ref, col):
    quarter = thick.shape[3]
    levels = 4 * quarter
    span = levels // 8
    row = lax.broadcasted_iota(jnp.int32, (levels, levels), 0)
    level = (row & 7) * span + lax.shift_right_logical(row, 3)
    j = lax.broadcasted_iota(jnp.int32, (levels, levels), 1)
    lower = (level >= j).astype(F32)
    at_level = level[:, :BLOCK].astype(F32) + 1.0
    low = jnp.zeros((1, 1), F32)
    high = jnp.zeros((1, 1), F32)
    for h in range(2):
        for s in range(4):
            col[h, s * quarter : (s + 1) * quarter, :] = thick[s, 0, h]
        upper = jnp.dot(lower, col[h], precision=HIGH, preferred_element_type=F32)
        e = upper * (levels / upper[levels - 1 :, :])
        e_ref[0, h] = e
        shift = e - at_level
        low = jnp.minimum(low, jnp.min(jnp.min(shift, axis=0, keepdims=True), axis=1, keepdims=True))
        high = jnp.maximum(high, jnp.max(jnp.max(shift, axis=0, keepdims=True), axis=1, keepdims=True))
    lo = jnp.maximum(-jnp.ceil(high), 1.0 - PAD).astype(jnp.int32)
    hi = jnp.minimum(-jnp.floor(low), PAD - 2.0 * RUN).astype(jnp.int32)
    n = lax.shift_right_logical(hi - lo + RUN, RUN.bit_length() - 1)
    lo_ref[0] = jnp.broadcast_to(lo, (1, BLOCK))
    n_ref[0] = jnp.broadcast_to(n, (1, BLOCK))


def edges(thick):
    _, rows, _, quarter, _ = thick.shape
    levels = 4 * quarter
    spec = pl.BlockSpec((4, 1, 2, quarter, BLOCK), lambda r: (0, r, 0, 0, 0))
    bound = jax.ShapeDtypeStruct((rows, 1, BLOCK), jnp.int32)
    bspec = pl.BlockSpec((1, 1, BLOCK), lambda r: (r, 0, 0))
    return pl.pallas_call(
        edges_kernel,
        grid=(rows,),
        in_specs=[spec],
        out_specs=[pl.BlockSpec((1, 2, levels, BLOCK), lambda r: (r, 0, 0, 0)), bspec, bspec],
        out_shape=[jax.ShapeDtypeStruct((rows, 2, levels, BLOCK), F32), bound, bound],
        scratch_shapes=[pltpu.VMEM((2, levels, BLOCK), F32)],
        compiler_params=params(24),
        cost_estimate=COST,
        name="edges",
    )(thick)


def remap_row(r, lo_ref, n_ref, e_ref, pieces, edge, cols, back, out):
    nf = cols.shape[0]
    quarter = pieces[0].shape[-2]
    levels = 4 * quarter
    span = levels // 8
    sub = lax.broadcasted_iota(jnp.int32, (8, BLOCK), 0)
    d0 = lo_ref[r, 0, 0]
    n = n_ref[r, 0, 0]

    def tile(ref, i):
        return ref[pl.ds(pl.multiple_of(i * 8, 8), 8), :]

    for h in range(2):
        edge[h, pl.ds(PAD * 8, levels), :] = e_ref[0, h]
        for k in range(4):
            src, s = (pieces[0].at[k], k) if len(pieces) == 1 else (pieces[k], lax.rem(lax.axis_index("lev") + 4 - k, 4))
            for m in range(quarter // 8):
                at = (PAD + 8 * (m % 2)) * 8 + m // 2 + s * (quarter // span)
                for f in range(nf):
                    cols[f, h, pl.ds(at, 8, stride=8), :] = src[f, 0, h, 8 * m : 8 * m + 8, :]

    def extend(i0, frm, turn, stop, fill):
        edge_row = sub == stop
        for t in range(RUN):
            i = i0 + t
            at = pl.ds(pl.multiple_of(i * 8, 8), 8)
            for h in range(2):
                edge[h, at, :] = jnp.where(edge_row, fill, pltpu.roll(tile(edge.at[h], i + frm), turn, 0))
                for f in range(nf):
                    cols[f, h, at, :] = jnp.where(edge_row, 0.0, pltpu.roll(tile(cols.at[f, h], i + frm), turn, 0))

    def above(k, c):
        extend(PAD + span + k * RUN, -span, 7, 7, 4.0 * levels)
        return c

    def below(k, c):
        extend(PAD - (k + 1) * RUN, span, 1, 0, 0.0)
        return c

    most = lax.shift_right_logical(jnp.maximum(d0 + n * RUN - 1, 0) + RUN - 1, RUN.bit_length() - 1)
    least = lax.shift_right_logical(jnp.maximum(-d0, 0) + RUN - 1, RUN.bit_length() - 1)
    lax.fori_loop(0, most, above, 0)
    lax.fori_loop(0, least, below, 0)

    spots = [(h, t) for h in range(2) for t in range(BUNCH)]
    many = len(spots)
    zero = jnp.zeros((8, BLOCK), F32)
    for g0 in range(0, span, BUNCH):
        lows = [(sub * span + (g0 + t)).astype(F32) for t in range(BUNCH)]
        highs = [x + 1.0 for x in lows]

        def some(k, carry):
            olds = list(carry[:many])
            accs = [list(carry[many * (f + 1) : many * (f + 2)]) for f in range(nf)]
            b = PAD + g0 + d0 + k * RUN
            for h in range(2):
                es = [tile(edge.at[h], b + x) for x in range(BUNCH + RUN - 1)]
                qs = [[tile(cols.at[f, h], b + x) for x in range(BUNCH + RUN - 1)] for f in range(nf)]
                for v in range(RUN):
                    for t in range(BUNCH):
                        i = h * BUNCH + t
                        p = jnp.minimum(jnp.maximum(es[v + t], lows[t]), highs[t])
                        w = p - olds[i]
                        olds[i] = p
                        for f in range(nf):
                            accs[f][i] = accs[f][i] + w * qs[f][v + t]
            return (*olds, *sum(accs, []))

        res = lax.fori_loop(0, n, some, (*lows, *lows) + (zero,) * (nf * many))
        for f in range(nf):
            for i, (h, t) in enumerate(spots):
                back[f, h, pl.ds(g0 + t, 8, stride=span), :] = res[many * (f + 1) + i]
    for f in range(nf):
        for h in range(2):
            out[f, 0, :, h * BLOCK : (h + 1) * BLOCK] = back[f, h]


def heat_kernel(lo_ref, n_ref, own_ref, day_ref, e_ref, exch, solar, *rest):
    *pieces, out, heating, shares, edge, cols, back = rest
    r = pl.program_id(0)
    remap_row(r, lo_ref, n_ref, e_ref, pieces, edge, cols, back, out)
    temp = out[0, 0]
    hum = out[1, 0]
    levels, width = temp.shape
    square = hum * hum
    clear = 1.0 / (1.0 + square)
    absorb = square * clear
    heat = jnp.dot(exch[0], absorb * temp, precision=HIGH, preferred_element_type=F32)
    heat = heat + jnp.dot(exch[1], clear * temp, precision=HIGH, preferred_element_type=F32)
    lane = lax.broadcasted_iota(jnp.int32, (1, width), 1)
    d0 = jnp.full((1, width), day_ref[2 * r], jnp.int32)
    d1 = jnp.full((1, width), day_ref[2 * r + 1], jnp.int32)
    day = jnp.where(lane < BLOCK, d0, d1).astype(F32)
    heat = heat + (day * solar[...]) * clear
    heating[0] = heat
    total = jnp.sum(heat, axis=0, keepdims=True)
    line = lax.broadcasted_iota(jnp.int32, (1, BLOCK), 1)

    @pl.when(r == 0)
    def _():
        shares[...] = jnp.zeros_like(shares)

    acc = shares[...]
    for b in range(2):
        mean = jnp.sum(total[:, b * BLOCK : (b + 1) * BLOCK], axis=1, keepdims=True) * (1.0 / (levels * BLOCK))
        acc = acc + jnp.where(line == own_ref[2 * r + b], mean, 0.0)
    shares[...] = acc


def remap_kernel(lo_ref, n_ref, e_ref, base, *rest):
    *pieces, out, edge, cols, back = rest
    remap_row(pl.program_id(0), lo_ref, n_ref, e_ref, pieces, edge, cols, back, out)


def remap(group, lo, n, e, pieces, base=None, heat_args=None):
    half, rows, _, quarter, _ = pieces[0].shape[-5:]
    levels = 4 * quarter
    width = 2 * BLOCK
    tall = levels + 2 * PAD * 8
    espec = pl.BlockSpec((1, 2, levels, BLOCK), lambda r: (r, 0, 0, 0))
    shape = (half, 1, 2, quarter, BLOCK)
    pspec = pl.BlockSpec(shape, lambda r: (0, r, 0, 0, 0))
    if len(pieces) == 1:
        pspec = pl.BlockSpec((4, *shape), lambda r: (0, 0, r, 0, 0, 0))
    pspecs = [pspec] * len(pieces)
    ospec = pl.BlockSpec((half, 1, levels, width), lambda r: (group, r, 0, 0))
    full = jax.ShapeDtypeStruct((2 * half, rows, levels, width), F32)
    common = dict(
        grid=(rows,),
        scratch_shapes=[
            pltpu.VMEM((2, tall, BLOCK), F32),
            pltpu.VMEM((half, 2, tall, BLOCK), F32),
            pltpu.VMEM((half, 2, levels, BLOCK), F32),
        ],
        compiler_params=params(24),
        cost_estimate=COST,
    )
    if heat_args is None:
        return pl.pallas_call(
            remap_kernel,
            in_specs=[SMEM, SMEM, espec, ANY] + pspecs,
            out_specs=ospec,
            out_shape=full,
            input_output_aliases={3: 0},
                name="remap",
            **common,
        )(lo, n, e, base, *pieces)
    owners, day, exchange, solar = heat_args
    hspec = pl.BlockSpec((1, levels, width), lambda r: (r, 0, 0))
    return pl.pallas_call(
        heat_kernel,
        in_specs=[SMEM, SMEM, SMEM, SMEM, espec]
        + [pl.BlockSpec((2, levels, levels), lambda r: (0, 0, 0)), pl.BlockSpec((levels, 1), lambda r: (0, 0))]
        + pspecs,
        out_specs=[ospec, hspec, pl.BlockSpec((1, BLOCK), lambda r: (0, 0))],
        out_shape=[full, jax.ShapeDtypeStruct((rows, levels, width), F32), jax.ShapeDtypeStruct((1, BLOCK), F32)],
        name="heat",
        **common,
    )(lo, n, owners, day, e, exchange, solar, *pieces)


def per_device(fields, thickness, courant_lon, courant_lat, exchange, solar_profile, owners, daylight):
    count = lax.axis_size("lat")
    ends = count - 1
    turn = lambda s: [(i, (i + s) % 4) for i in range(4)]
    around = lambda ps: [ps[0]] + [lax.ppermute(p, "lev", turn(s + 1)) for s, p in enumerate(ps[1:])]
    regroup = lambda x: lax.all_to_all(x, "lev", split_axis=0, concat_axis=0, tiled=True)

    head, tail, thick = prep(fields, courant_lon, thickness)
    prev = lax.ppermute(tail, "lat", [(i, i + 1) for i in range(ends)])
    nxt = lax.ppermute(head, "lat", [(i + 1, i) for i in range(ends)])
    e, lo, n = edges(regroup(thick))
    first = advect(0, fields, courant_lon, courant_lat, prev, nxt, True, head)
    second = around(advect(1, fields, courant_lon, courant_lat, prev, nxt, False, first[0]))
    first = [regroup(first[0])]
    heat_args = (owners[:, 0], daylight, exchange, solar_profile[:, None])
    remapped, heating, shares = remap(0, lo, n, e, first, heat_args=heat_args)
    remapped = remap(1, lo, n, e, second, base=remapped)
    shares = shares[0, :count].reshape(count, 1, 1)
    owner_heat = jnp.sum(lax.all_to_all(shares, "lat", split_axis=0, concat_axis=0, tiled=True)).reshape(1, 1)
    return (remapped, heating, owner_heat)


def solution(mesh):
    placed = (
        P(None, "lat", "lev", None),
        P("lat", "lev", None),
        P("lat", "lev", None),
        P("lat", "lev", None),
        P(),
        P(),
        P(("lat", "lev"), None),
        P(("lat", "lev")),
    )
    return jax.shard_map(
        per_device,
        mesh=mesh,
        in_specs=placed,
        out_specs=(P(None, "lat", None, "lev"), P("lat", None, "lev"), P("lat", "lev")),
        check_vma=False,
    )
```

```python
import functools

import jax
import jax.numpy as jnp
from jax import lax
from jax.experimental import pallas as pl
from jax.experimental.pallas import tpu as pltpu
from jax.sharding import PartitionSpec as P

F32 = jnp.float32
HIGH = lax.Precision.HIGHEST
ANY = pl.BlockSpec(memory_space=pl.ANY)
SMEM = pl.BlockSpec(memory_space=pltpu.SMEM)
BLOCK = 128
PAD = 48
RUN = 4
BUNCH = 4
MIB = 1024 * 1024


COST = pl.CostEstimate(flops=1, bytes_accessed=1, transcendentals=0)


def params(mib):
    return pltpu.CompilerParams(vmem_limit_bytes=mib * MIB)


def coefs(c):
    sq = 0.5 * c * c
    half = 0.5 * c
    return 1.0 - 2.0 * sq, sq - half, sq + half


def lon_step(x, w):
    n = x.shape[-1]
    mid, up, down = w
    return mid * x + up * pltpu.roll(x, n - 1, 1) + down * pltpu.roll(x, 1, 1)


def put(sent, k, r, value):
    for d in range(4):
        for h in range(2):
            at = (2 * d + h) * BLOCK
            sent[d, k, r, h] = value[:, at : at + BLOCK]


def inner_kernel(q, head_in, tail_in, c_lon, c_lat, thick, head, tail, *rest):
    *sent, keep, sems = rest
    step = pl.program_id(0)
    last = pl.num_programs(0) - 1
    nf, rows = q.shape[0], q.shape[1]

    def copies(k):
        return turned(sent, lambda cols: keep.at[k, :, :, :, cols], sems, k)

    before = here = None
    for r in range(rows):
        w = coefs(c_lon[r])
        ahead = [lon_step(q[f, r], w) for f in range(nf)]
        if r in (0, rows - 1):
            src, dst = (head_in, head) if r == 0 else (tail_in, tail)
            for f in range(nf):
                dst[f] = ahead[f]
                dst[nf + f] = lon_step(src[f, 0], w)
        else:
            keep[step, 0, r - 1] = thick[r]
        if r > 1:
            mid, up, down = coefs(c_lat[r - 1])
            for f in range(nf):
                keep[step, 1 + f, r - 2] = mid * here[f] + up * ahead[f] + down * before[f]
        before, here = here, ahead
    for c in copies(step):
        c.start()

    @pl.when(step == last)
    def _():
        for k in range(4):
            for c in copies(k):
                c.wait()


def inner(fields, c_lon, c_lat, thickness):
    nf, rows, levs, lon = fields.shape
    half = nf // 2
    cspec = pl.BlockSpec((rows, 8, lon), lambda i: (0, i, 0))
    edge = lambda r: pl.BlockSpec((half, 1, 8, lon), lambda i: (1, r, i, 0))
    ospec = pl.BlockSpec((nf, 8, lon), lambda i: (0, i, 0))
    side = pltpu.HBM((nf, levs, lon), F32)
    return pl.pallas_call(
        inner_kernel,
        grid=(levs // 8,),
        in_specs=[pl.BlockSpec((half, rows, 8, lon), lambda i: (0, 0, i, 0)), edge(0), edge(rows - 1)] + [cspec] * 3,
        out_specs=[ospec, ospec] + [ANY] * 4,
        out_shape=[side, side] + [pltpu.HBM((1 + half, rows - 2, 2, levs, BLOCK), F32)] * 4,
        scratch_shapes=[
            pltpu.VMEM((levs // 8, 1 + half, rows - 2, 8, lon), F32),
            pltpu.SemaphoreType.DMA((levs // 8, 4, 2)),
        ],
        compiler_params=params(12),
        cost_estimate=COST,
        name="inner",
    )(fields, fields, fields, c_lon, c_lat, thickness)


def outer_kernel(head, tail, q1, q2, c1, c2, l1, l2, th1, th2, prev, nxt, sent):
    nf = head.shape[0]
    for e, (here, q, c, lat, th) in enumerate(((head, q1, c1, l1, th1), (tail, q2, c2, l2, th2))):
        put(sent, 0, e, th[0])
        w = coefs(c[0])
        mid, up, down = coefs(lat[0])
        for f in range(nf):
            beside = lon_step(q[f, 0], w)
            before, ahead = (prev[f], beside) if e == 0 else (beside, nxt[f])
            put(sent, 1 + f, e, mid * here[f] + up * ahead + down * before)


def outer(head, tail, fields, c_lon, c_lat, thickness, prev, nxt):
    nf, rows, levs, lon = fields.shape
    half = nf // 2
    steps = levs // 8
    sspec = pl.BlockSpec((half, 8, lon), lambda i: (0, i, 0))
    qrow = lambda r: pl.BlockSpec((half, 1, 8, lon), lambda i: (0, r, i, 0))
    crow = lambda r: pl.BlockSpec((1, 8, lon), lambda i: (r, i, 0))
    end = rows - 1
    return pl.pallas_call(
        outer_kernel,
        grid=(steps,),
        in_specs=[sspec, sspec, qrow(1), qrow(end - 1), crow(1), crow(end - 1)]
        + [crow(0), crow(end)] * 2
        + [sspec, sspec],
        out_specs=pl.BlockSpec((4, 1 + half, 2, 2, 8, BLOCK), lambda i: (0, 0, 0, 0, i, 0)),
        out_shape=pltpu.HBM((4, 1 + half, 2, 2, levs, BLOCK), F32),
        compiler_params=params(12),
        cost_estimate=COST,
        name="outer",
    )(head, tail, fields, fields, c_lon, c_lon, c_lat, c_lat, thickness, thickness, prev, nxt)


def turned(sent, part, sems, k):
    out = []
    for s, dst in enumerate(sent):
        for h in range(2):
            at = pl.multiple_of(lax.rem(lax.axis_index("lev") + s, 4) * (2 * BLOCK) + h * BLOCK, BLOCK)
            lev = pl.multiple_of(k * 8, 8)
            out.append(
                pltpu.make_async_copy(part(pl.ds(at, BLOCK)), dst.at[:, :, h, pl.ds(lev, 8), :], sems.at[k, s, h])
            )
    return out


def advect_kernel(q, c_lon, c_lat, prev, nxt, *rest):
    *sent, keep, sems = rest
    step = pl.program_id(0)
    last = pl.num_programs(0) - 1
    nf, rows = q.shape[0], q.shape[1]

    def copies(k):
        return turned(sent, lambda cols: keep.at[k, :, :, :, cols], sems, k)

    before = [prev[f] for f in range(nf)]
    w = coefs(c_lon[0])
    here = [lon_step(q[f, 0], w) for f in range(nf)]
    for r in range(rows):
        if r + 1 < rows:
            w = coefs(c_lon[r + 1])
            ahead = [lon_step(q[f, r + 1], w) for f in range(nf)]
        else:
            ahead = [nxt[f] for f in range(nf)]
        mid, up, down = coefs(c_lat[r])
        for f in range(nf):
            keep[step, f, r] = mid * here[f] + up * ahead[f] + down * before[f]
        before, here = here, ahead
    for c in copies(step):
        c.start()

    @pl.when(step == last)
    def _():
        for k in range(4):
            for c in copies(k):
                c.wait()


def advect(group, fields, c_lon, c_lat, prev, nxt):
    nf, rows, levs, lon = fields.shape
    half = nf // 2
    steps = levs // 8
    cspec = pl.BlockSpec((rows, 8, lon), lambda i: (0, i, 0))
    hspec = pl.BlockSpec((half, 8, lon), lambda i: (group, i, 0))
    shape = (half, rows, 2, levs, BLOCK)
    piece = [pltpu.HBM(shape, F32)] * 4
    return pl.pallas_call(
        advect_kernel,
        grid=(steps,),
        in_specs=[pl.BlockSpec((half, rows, 8, lon), lambda i: (group, 0, i, 0)), cspec, cspec, hspec, hspec],
        out_specs=[ANY] * len(piece),
        out_shape=piece,
        scratch_shapes=[pltpu.VMEM((steps, half, rows, 8, lon), F32), pltpu.SemaphoreType.DMA((steps, 4, 2))],
        compiler_params=params(12),
        cost_estimate=COST,
        name="advect",
    )(fields, c_lon, c_lat, prev, nxt)


def source(pieces, k):
    if len(pieces) == 1:
        return pieces[0].at[k], k
    return pieces[k], lax.rem(lax.axis_index("lev") + 4 - k, 4)


def remap_row(d0, n, e_ref, pieces, first, edge, cols, back, out):
    nf = cols.shape[0]
    quarter = pieces[0].shape[-2]
    levels = 4 * quarter
    span = levels // 8
    sub = lax.broadcasted_iota(jnp.int32, (8, BLOCK), 0)

    def tile(ref, i):
        return ref[pl.ds(pl.multiple_of(i * 8, 8), 8), :]

    for h in range(2):
        edge[h, pl.ds(PAD * 8, levels), :] = e_ref[0, h]
        for k in range(4):
            src, s = source(pieces, k)
            for m in range(quarter // 8):
                at = (PAD + 8 * (m % 2)) * 8 + m // 2 + s * (quarter // span)
                for f in range(nf):
                    cols[f, h, pl.ds(at, 8, stride=8), :] = src[first + f, 0, h, 8 * m : 8 * m + 8, :]

    def extend(i0, frm, turn, stop, fill):
        edge_row = sub == stop
        for t in range(RUN):
            i = i0 + t
            at = pl.ds(pl.multiple_of(i * 8, 8), 8)
            for h in range(2):
                edge[h, at, :] = jnp.where(edge_row, fill, pltpu.roll(tile(edge.at[h], i + frm), turn, 0))
                for f in range(nf):
                    cols[f, h, at, :] = jnp.where(edge_row, 0.0, pltpu.roll(tile(cols.at[f, h], i + frm), turn, 0))

    def above(k, c):
        extend(PAD + span + k * RUN, -span, 7, 7, 4.0 * levels)
        return c

    def below(k, c):
        extend(PAD - (k + 1) * RUN, span, 1, 0, 0.0)
        return c

    most = lax.shift_right_logical(jnp.maximum(d0 + n * RUN - 1, 0) + RUN - 1, RUN.bit_length() - 1)
    least = lax.shift_right_logical(jnp.maximum(-d0, 0) + RUN - 1, RUN.bit_length() - 1)
    lax.fori_loop(0, most, above, 0)
    lax.fori_loop(0, least, below, 0)

    spots = [(h, t) for h in range(2) for t in range(BUNCH)]
    many = len(spots)
    zero = jnp.zeros((8, BLOCK), F32)
    for g0 in range(0, span, BUNCH):
        lows = [(sub * span + (g0 + t)).astype(F32) for t in range(BUNCH)]
        highs = [x + 1.0 for x in lows]

        def some(k, carry):
            olds = list(carry[:many])
            accs = [list(carry[many * (f + 1) : many * (f + 2)]) for f in range(nf)]
            b = PAD + g0 + d0 + k * RUN
            for h in range(2):
                es = [tile(edge.at[h], b + x) for x in range(BUNCH + RUN - 1)]
                qs = [[tile(cols.at[f, h], b + x) for x in range(BUNCH + RUN - 1)] for f in range(nf)]
                for v in range(RUN):
                    for t in range(BUNCH):
                        i = h * BUNCH + t
                        p = jnp.minimum(jnp.maximum(es[v + t], lows[t]), highs[t])
                        w = p - olds[i]
                        olds[i] = p
                        for f in range(nf):
                            accs[f][i] = accs[f][i] + w * qs[f][v + t]
            return (*olds, *sum(accs, []))

        res = lax.fori_loop(0, n, some, (*lows, *lows) + (zero,) * (nf * many))
        for f in range(nf):
            for i, (h, t) in enumerate(spots):
                back[f, h, pl.ds(g0 + t, 8, stride=span), :] = res[many * (f + 1) + i]
    for f in range(nf):
        for h in range(2):
            out[f, 0, :, h * BLOCK : (h + 1) * BLOCK] = back[f, h]


def edges_row(pieces, col, e_ref):
    quarter = pieces[0].shape[-2]
    levels = 4 * quarter
    row = lax.broadcasted_iota(jnp.int32, (levels, levels), 0)
    level = (row & 7) * (levels // 8) + lax.shift_right_logical(row, 3)
    j = lax.broadcasted_iota(jnp.int32, (levels, levels), 1)
    lower = (level >= j).astype(F32)
    at_level = level[:, :BLOCK].astype(F32) + 1.0
    low = jnp.zeros((1, 1), F32)
    high = jnp.zeros((1, 1), F32)
    for h in range(2):
        for k in range(4):
            src, s = source(pieces, k)
            at = s * quarter if isinstance(s, int) else pl.multiple_of(s * quarter, quarter)
            col[h, pl.ds(at, quarter), :] = src[0, 0, h]
        upper = jnp.dot(lower, col[h], precision=HIGH, preferred_element_type=F32)
        e = upper * (levels / upper[levels - 1 :, :])
        e_ref[0, h] = e
        shift = e - at_level
        low = jnp.minimum(low, jnp.min(jnp.min(shift, axis=0, keepdims=True), axis=1, keepdims=True))
        high = jnp.maximum(high, jnp.max(jnp.max(shift, axis=0, keepdims=True), axis=1, keepdims=True))
    lo = jnp.maximum(-jnp.ceil(high), 1.0 - PAD).astype(jnp.int32)
    hi = jnp.minimum(-jnp.floor(low), PAD - 2.0 * RUN).astype(jnp.int32)
    n = lax.shift_right_logical(hi - lo + RUN, RUN.bit_length() - 1)
    return lo[0, 0], n[0, 0]


def halves(x):
    top = x.astype(jnp.bfloat16)
    return top, (x - top.astype(F32)).astype(jnp.bfloat16)


def heat_kernel(row_of, skip, own_ref, day_ref, exch, solar, so_far, *rest):
    *pieces, out, heating, shares, e_ref, lo_ref, n_ref, edge, cols, back, col, mats = rest
    pieces = pieces[skip:]
    step = pl.program_id(0)
    r = row_of(step)

    @pl.when(step == 0)
    def _():
        shares[...] = so_far[...]
        both = jnp.concatenate([exch[0], exch[1]], axis=1)
        mats[0], mats[1] = halves(both)

    d0, n = edges_row(pieces, col, e_ref)
    lo_ref[step] = d0
    n_ref[step] = n
    remap_row(d0, n, e_ref, pieces, 1, edge, cols, back, out)
    temp = out[0, 0]
    hum = out[1, 0]
    levels, width = temp.shape
    square = hum * hum
    clear = 1.0 / (1.0 + square)
    absorb = square * clear
    top, rest_of = halves(jnp.concatenate([absorb * temp, clear * temp], axis=0))
    heat = jnp.dot(mats[0], rest_of, preferred_element_type=F32) + jnp.dot(mats[1], top, preferred_element_type=F32)
    heat = heat + jnp.dot(mats[0], top, preferred_element_type=F32)
    lane = lax.broadcasted_iota(jnp.int32, (1, width), 1)
    d0 = jnp.full((1, width), day_ref[2 * r], jnp.int32)
    d1 = jnp.full((1, width), day_ref[2 * r + 1], jnp.int32)
    day = jnp.where(lane < BLOCK, d0, d1).astype(F32)
    heat = heat + (day * solar[...]) * clear
    heating[0] = heat
    total = jnp.sum(heat, axis=0, keepdims=True)
    line = lax.broadcasted_iota(jnp.int32, (1, BLOCK), 1)
    acc = shares[...]
    for b in range(2):
        mean = jnp.sum(total[:, b * BLOCK : (b + 1) * BLOCK], axis=1, keepdims=True) * (1.0 / (levels * BLOCK))
        acc = acc + jnp.where(line == own_ref[2 * r + b], mean, 0.0)
    shares[...] = acc


def piece_spec(pieces):
    many, _, _, quarter, _ = pieces[0].shape[-5:]
    shape = (many, 1, 2, quarter, BLOCK)
    if len(pieces) == 1:
        return [pl.BlockSpec((4, *shape), lambda r: (0, 0, r, 0, 0, 0))]
    return [pl.BlockSpec(shape, lambda r: (0, r, 0, 0, 0))] * 4


def row_scratch(levels, half):
    tall = levels + 2 * PAD * 8
    return [
        pltpu.VMEM((2, tall, BLOCK), F32),
        pltpu.VMEM((half, 2, tall, BLOCK), F32),
        pltpu.VMEM((half, 2, levels, BLOCK), F32),
    ]


def heat(pieces, rows, row_of, owners, day, exchange, solar, shares, made=()):
    many, count, _, quarter, _ = pieces[0].shape[-5:]
    half = many - 1
    levels = 4 * quarter
    width = 2 * BLOCK
    bound = jax.ShapeDtypeStruct((count,), jnp.int32)
    whole = pl.BlockSpec((1, BLOCK), lambda r: (0, 0))
    return pl.pallas_call(
        functools.partial(heat_kernel, row_of, len(made)),
        grid=(count,),
        in_specs=[
            SMEM,
            SMEM,
            pl.BlockSpec((2, levels, levels), lambda r: (0, 0, 0)),
            pl.BlockSpec((levels, 1), lambda r: (0, 0)),
            whole,
        ]
        + [ANY] * len(made)
        + piece_spec(pieces),
        out_specs=[
            pl.BlockSpec((half, 1, levels, width), lambda r: (0, row_of(r), 0, 0)),
            pl.BlockSpec((1, levels, width), lambda r: (row_of(r), 0, 0)),
            whole,
            pl.BlockSpec((1, 2, levels, BLOCK), lambda r: (row_of(r), 0, 0, 0)),
            SMEM,
            SMEM,
        ],
        out_shape=[
            jax.ShapeDtypeStruct((2 * half, rows, levels, width), F32),
            jax.ShapeDtypeStruct((rows, levels, width), F32),
            jax.ShapeDtypeStruct((1, BLOCK), F32),
            jax.ShapeDtypeStruct((rows, 2, levels, BLOCK), F32),
            bound,
            bound,
        ],
        input_output_aliases={5: 0, 6: 1, 7: 3} if made else {},
        scratch_shapes=row_scratch(levels, half)
        + [pltpu.VMEM((2, levels, BLOCK), F32), pltpu.VMEM((2, levels, 2 * levels), jnp.bfloat16)],
        compiler_params=params(12),
        cost_estimate=COST,
        name="heat",
    )(owners, day, exchange, solar, shares, *made, *pieces)


def remap_kernel(lo_in, n_in, lo_out, n_out, e_ref, base, *rest):
    *pieces, out, edge, cols, back = rest
    r = pl.program_id(0)
    end = pl.num_programs(0) - 1
    rim = jnp.logical_or(r == 0, r == end)
    at = jnp.clip(r - 1, 0, end - 2)
    side = jnp.minimum(r, 1)
    d0 = jnp.where(rim, lo_out[side], lo_in[at])
    n = jnp.where(rim, n_out[side], n_in[at])
    remap_row(d0, n, e_ref, pieces, 0, edge, cols, back, out)


def remap(inside, outside, e, pieces, base):
    half, rows, _, quarter, _ = pieces[0].shape[-5:]
    levels = 4 * quarter
    width = 2 * BLOCK
    return pl.pallas_call(
        remap_kernel,
        grid=(rows,),
        in_specs=[SMEM] * 4 + [pl.BlockSpec((1, 2, levels, BLOCK), lambda r: (r, 0, 0, 0)), ANY] + piece_spec(pieces),
        out_specs=pl.BlockSpec((half, 1, levels, width), lambda r: (1, r, 0, 0)),
        out_shape=jax.ShapeDtypeStruct((2 * half, rows, levels, width), F32),
        input_output_aliases={5: 0},
        scratch_shapes=row_scratch(levels, half),
        compiler_params=params(12),
        cost_estimate=COST,
        name="remap",
    )(*inside, *outside, e, base, *pieces)


def per_device(fields, thickness, courant_lon, courant_lat, exchange, solar_profile, owners, daylight):
    count = lax.axis_size("lat")
    rows = fields.shape[1]
    ends = count - 1
    hbm = lambda xs: [pltpu.with_memory_space_constraint(x, pltpu.HBM) for x in xs]
    turn = lambda s: [(i, (i + s) % 4) for i in range(4)]
    around = lambda ps: hbm(ps[:1]) + [lax.ppermute(p, "lev", turn(s + 1)) for s, p in enumerate(ps[1:])]
    regroup = lambda x: lax.all_to_all(x, "lev", split_axis=0, concat_axis=0, tiled=True)

    fields, thickness, courant_lon, courant_lat = hbm([fields, thickness, courant_lon, courant_lat])
    head, tail, *inside = inner(fields, courant_lon, courant_lat, thickness)
    prev = lax.ppermute(tail, "lat", [(i, i + 1) for i in range(ends)])
    nxt = lax.ppermute(head, "lat", [(i + 1, i) for i in range(ends)])
    inside = around(inside)
    head, tail = hbm([head, tail])
    outside = [regroup(outer(head, tail, fields, courant_lon, courant_lat, thickness, prev, nxt))]
    second = around(advect(1, fields, courant_lon, courant_lat, prev, nxt))

    other = (owners[:, 0], daylight, exchange, solar_profile[:, None])
    shares = jnp.zeros((1, BLOCK), F32)
    remapped, heating, shares, e, *inside = heat(inside, rows, lambda r: r + 1, *other, shares)
    made = (remapped, heating, e)
    remapped, heating, shares, e, *outside = heat(outside, rows, lambda r: r * (rows - 1), *other, shares, made)
    remapped = remap(inside, outside, e, second, remapped)
    shares = shares[0, :count].reshape(count, 1, 1)
    owner_heat = jnp.sum(lax.all_to_all(shares, "lat", split_axis=0, concat_axis=0, tiled=True)).reshape(1, 1)
    return (remapped, heating, owner_heat)


def solution(mesh):
    placed = (
        P(None, "lat", "lev", None),
        P("lat", "lev", None),
        P("lat", "lev", None),
        P("lat", "lev", None),
        P(),
        P(),
        P(("lat", "lev"), None),
        P(("lat", "lev")),
    )
    return jax.shard_map(
        per_device,
        mesh=mesh,
        in_specs=placed,
        out_specs=(P(None, "lat", None, "lev"), P("lat", None, "lev"), P("lat", "lev")),
        check_vma=False,
    )
```

```python
import functools

import jax
import jax.numpy as jnp
from jax import lax
from jax.experimental import pallas as pl
from jax.experimental.pallas import tpu as pltpu
from jax.sharding import PartitionSpec as P

F32 = jnp.float32
HIGH = lax.Precision.HIGHEST
ANY = pl.BlockSpec(memory_space=pl.ANY)
SMEM = pl.BlockSpec(memory_space=pltpu.SMEM)
BLOCK = 128
PAD = 48
RUN = 4
BUNCH = 4
MIB = 1024 * 1024


COST = pl.CostEstimate(flops=1, bytes_accessed=1, transcendentals=0)


def params(mib):
    return pltpu.CompilerParams(vmem_limit_bytes=mib * MIB)


def coefs(c):
    sq = 0.5 * c * c
    half = 0.5 * c
    return 1.0 - 2.0 * sq, sq - half, sq + half


def lon_step(x, w):
    n = x.shape[-1]
    mid, up, down = w
    return mid * x + up * pltpu.roll(x, n - 1, 1) + down * pltpu.roll(x, 1, 1)


def put(sent, k, r, value):
    for d in range(4):
        for h in range(2):
            at = (2 * d + h) * BLOCK
            sent[d, k, r, h] = value[:, at : at + BLOCK]


def staged(ins, outs, sems, body):
    def reads(k):
        return [pltpu.make_async_copy(part(k), buf.at[k], sems.at[k, i]) for i, (part, buf) in enumerate(ins)]

    steps = ins[0][1].shape[0]
    for k in range(steps):
        for c in reads(k):
            c.start()

    def step(k, carry):
        for c in reads(k):
            c.wait()
        body(k, [buf.at[k] for _, buf in ins])
        for c in outs(k):
            c.start()
        return carry

    lax.fori_loop(0, steps, step, 0)
    for k in range(steps):
        for c in outs(k):
            c.wait()


def levs_of(k):
    return pl.ds(pl.multiple_of(k * 8, 8), 8)


def spread_kernel(thick, sent, buf, in_sems, sems):
    def outs(k):
        out = []
        for d in range(4):
            for h in range(2):
                at = (2 * d + h) * BLOCK
                out.append(
                    pltpu.make_async_copy(
                        buf.at[k, :, :, pl.ds(at, BLOCK)], sent.at[d, :, h, levs_of(k), :], sems.at[k, d, h]
                    )
                )
        return out

    staged([(lambda k: thick.at[:, levs_of(k), :], buf)], outs, in_sems, lambda k, bufs: None)


def spread(thickness):
    rows, levs, lon = thickness.shape
    steps = levs // 8
    return pl.pallas_call(
        spread_kernel,
        in_specs=[ANY],
        out_specs=ANY,
        out_shape=pltpu.HBM((4, rows, 2, levs, BLOCK), F32),
        scratch_shapes=[
            pltpu.VMEM((steps, rows, 8, lon), F32),
            pltpu.SemaphoreType.DMA((steps, 1)),
            pltpu.SemaphoreType.DMA((steps, 4, 2)),
        ],
        compiler_params=params(8),
        cost_estimate=COST,
        name="spread",
    )(thickness)


def inner_kernel(fields, c_lon, c_lat, after, head, tail, *rest):
    *sent, q_b, h_b, t_b, lon_b, lat_b, keep, ends, in_sems, sems, end_sems = rest
    nf, rows = q_b.shape[1], q_b.shape[2]
    ins = [
        (lambda k: fields.at[:nf, :, levs_of(k), :], q_b),
        (lambda k: c_lon.at[:, levs_of(k), :], lon_b),
        (lambda k: fields.at[nf:, 0, levs_of(k), :], h_b),
        (lambda k: fields.at[nf:, rows - 1, levs_of(k), :], t_b),
        (lambda k: c_lat.at[:, levs_of(k), :], lat_b),
    ]

    def outs(k):
        out = turned(sent, lambda cols: keep.at[k, :, :, :, cols], sems, k)
        for e, dst in enumerate((head, tail)):
            out.append(pltpu.make_async_copy(ends.at[k, e], dst.at[:, levs_of(k), :], end_sems.at[k, e]))
        return out

    def body(k, bufs):
        q, lon, head_in, tail_in, lat = bufs
        before = here = None
        for r in range(rows):
            w = coefs(lon[r])
            ahead = [lon_step(q[f, r], w) for f in range(nf)]
            if r in (0, rows - 1):
                e, src = (0, head_in) if r == 0 else (1, tail_in)
                for f in range(nf):
                    ends[k, e, f] = ahead[f]
                    ends[k, e, nf + f] = lon_step(src[f], w)
            if r > 1:
                mid, up, down = coefs(lat[r - 1])
                for f in range(nf):
                    keep[k, f, r - 2] = mid * here[f] + up * ahead[f] + down * before[f]
            before, here = here, ahead

    staged(ins, outs, in_sems, body)


def inner(fields, c_lon, c_lat, after):
    nf, rows, levs, lon = fields.shape
    half = nf // 2
    steps = levs // 8
    side = pltpu.HBM((nf, levs, lon), F32)
    sem = pltpu.SemaphoreType.DMA
    return pl.pallas_call(
        inner_kernel,
        in_specs=[ANY] * 4,
        out_specs=[ANY] * 6,
        out_shape=[side, side] + [pltpu.HBM((half, rows - 2, 2, levs, BLOCK), F32)] * 4,
        scratch_shapes=[
            pltpu.VMEM((steps, half, rows, 8, lon), F32),
            pltpu.VMEM((steps, half, 8, lon), F32),
            pltpu.VMEM((steps, half, 8, lon), F32),
            pltpu.VMEM((steps, rows, 8, lon), F32),
            pltpu.VMEM((steps, rows, 8, lon), F32),
            pltpu.VMEM((steps, half, rows - 2, 8, lon), F32),
            pltpu.VMEM((steps, 2, nf, 8, lon), F32),
            sem((steps, 5)),
            sem((steps, 4, 2)),
            sem((steps, 2)),
        ],
        compiler_params=params(20),
        cost_estimate=COST,
        name="inner",
    )(fields, c_lon, c_lat, after)


def outer_kernel(head, tail, q1, q2, c1, c2, l1, l2, prev, nxt, after, sent):
    nf = head.shape[0]
    for e, (here, q, c, lat) in enumerate(((head, q1, c1, l1), (tail, q2, c2, l2))):
        w = coefs(c[0])
        mid, up, down = coefs(lat[0])
        for f in range(nf):
            beside = lon_step(q[f, 0], w)
            before, ahead = (prev[f], beside) if e == 0 else (beside, nxt[f])
            put(sent, f, e, mid * here[f] + up * ahead + down * before)


def outer(head, tail, fields, c_lon, c_lat, prev, nxt, after):
    nf, rows, levs, lon = fields.shape
    half = nf // 2
    steps = levs // 8
    sspec = pl.BlockSpec((half, 8, lon), lambda i: (0, i, 0))
    qrow = lambda r: pl.BlockSpec((half, 1, 8, lon), lambda i: (0, r, i, 0))
    crow = lambda r: pl.BlockSpec((1, 8, lon), lambda i: (r, i, 0))
    end = rows - 1
    return pl.pallas_call(
        outer_kernel,
        grid=(steps,),
        in_specs=[sspec, sspec, qrow(1), qrow(end - 1), crow(1), crow(end - 1)]
        + [crow(0), crow(end), sspec, sspec, ANY],
        out_specs=pl.BlockSpec((4, half, 2, 2, 8, BLOCK), lambda i: (0, 0, 0, 0, i, 0)),
        out_shape=pltpu.HBM((4, half, 2, 2, levs, BLOCK), F32),
        compiler_params=params(12),
        cost_estimate=COST,
        name="outer",
    )(head, tail, fields, fields, c_lon, c_lon, c_lat, c_lat, prev, nxt, after)


def turned(sent, part, sems, k):
    out = []
    for s, dst in enumerate(sent):
        for h in range(2):
            at = pl.multiple_of(lax.rem(lax.axis_index("lev") + s, 4) * (2 * BLOCK) + h * BLOCK, BLOCK)
            lev = pl.multiple_of(k * 8, 8)
            out.append(
                pltpu.make_async_copy(part(pl.ds(at, BLOCK)), dst.at[:, :, h, pl.ds(lev, 8), :], sems.at[k, s, h])
            )
    return out


def advect_kernel(group, fields, c_lon, c_lat, prev, nxt, *rest):
    *sent, q_b, lon_b, lat_b, prev_b, nxt_b, keep, in_sems, sems = rest
    nf, rows = q_b.shape[1], q_b.shape[2]
    which = slice(group * nf, (group + 1) * nf)
    ins = [
        (lambda k: fields.at[which, :, levs_of(k), :], q_b),
        (lambda k: c_lon.at[:, levs_of(k), :], lon_b),
        (lambda k: c_lat.at[:, levs_of(k), :], lat_b),
        (lambda k: prev.at[which, levs_of(k), :], prev_b),
        (lambda k: nxt.at[which, levs_of(k), :], nxt_b),
    ]

    def outs(k):
        return turned(sent, lambda cols: keep.at[k, :, :, :, cols], sems, k)

    def body(k, bufs):
        q, lon, lat, prev_in, nxt_in = bufs
        before = [prev_in[f] for f in range(nf)]
        w = coefs(lon[0])
        here = [lon_step(q[f, 0], w) for f in range(nf)]
        for r in range(rows):
            if r + 1 < rows:
                w = coefs(lon[r + 1])
                ahead = [lon_step(q[f, r + 1], w) for f in range(nf)]
            else:
                ahead = [nxt_in[f] for f in range(nf)]
            mid, up, down = coefs(lat[r])
            for f in range(nf):
                keep[k, f, r] = mid * here[f] + up * ahead[f] + down * before[f]
            before, here = here, ahead

    staged(ins, outs, in_sems, body)


def advect(group, fields, c_lon, c_lat, prev, nxt):
    nf, rows, levs, lon = fields.shape
    half = nf // 2
    steps = levs // 8
    sem = pltpu.SemaphoreType.DMA
    return pl.pallas_call(
        functools.partial(advect_kernel, group),
        in_specs=[ANY] * 5,
        out_specs=[ANY] * 4,
        out_shape=[pltpu.HBM((half, rows, 2, levs, BLOCK), F32)] * 4,
        scratch_shapes=[
            pltpu.VMEM((steps, half, rows, 8, lon), F32),
            pltpu.VMEM((steps, rows, 8, lon), F32),
            pltpu.VMEM((steps, rows, 8, lon), F32),
            pltpu.VMEM((steps, half, 8, lon), F32),
            pltpu.VMEM((steps, half, 8, lon), F32),
            pltpu.VMEM((steps, half, rows, 8, lon), F32),
            sem((steps, 5)),
            sem((steps, 4, 2)),
        ],
        compiler_params=params(20),
        cost_estimate=COST,
        name="advect",
    )(fields, c_lon, c_lat, prev, nxt)


def source(pieces, k):
    if len(pieces) == 1:
        return pieces[0].at[k], k
    return pieces[k], lax.rem(lax.axis_index("lev") + 4 - k, 4)


def remap_row(d0, n, e_ref, pieces, edge, cols, back, out):
    nf = cols.shape[0]
    quarter = pieces[0].shape[-2]
    levels = 4 * quarter
    span = levels // 8
    sub = lax.broadcasted_iota(jnp.int32, (8, BLOCK), 0)

    def tile(ref, i):
        return ref[pl.ds(pl.multiple_of(i * 8, 8), 8), :]

    for h in range(2):
        edge[h, pl.ds(PAD * 8, levels), :] = e_ref[0, h]
        for k in range(4):
            src, s = source(pieces, k)
            for m in range(quarter // 8):
                at = (PAD + 8 * (m % 2)) * 8 + m // 2 + s * (quarter // span)
                for f in range(nf):
                    cols[f, h, pl.ds(at, 8, stride=8), :] = src[f, 0, h, 8 * m : 8 * m + 8, :]

    def extend(i0, frm, turn, stop, fill):
        edge_row = sub == stop
        for t in range(RUN):
            i = i0 + t
            at = pl.ds(pl.multiple_of(i * 8, 8), 8)
            for h in range(2):
                edge[h, at, :] = jnp.where(edge_row, fill, pltpu.roll(tile(edge.at[h], i + frm), turn, 0))
                for f in range(nf):
                    cols[f, h, at, :] = jnp.where(edge_row, 0.0, pltpu.roll(tile(cols.at[f, h], i + frm), turn, 0))

    def above(k, c):
        extend(PAD + span + k * RUN, -span, 7, 7, 4.0 * levels)
        return c

    def below(k, c):
        extend(PAD - (k + 1) * RUN, span, 1, 0, 0.0)
        return c

    most = lax.shift_right_logical(jnp.maximum(d0 + n * RUN - 1, 0) + RUN - 1, RUN.bit_length() - 1)
    least = lax.shift_right_logical(jnp.maximum(-d0, 0) + RUN - 1, RUN.bit_length() - 1)
    lax.fori_loop(0, most, above, 0)
    lax.fori_loop(0, least, below, 0)

    spots = [(h, t) for h in range(2) for t in range(BUNCH)]
    many = len(spots)
    zero = jnp.zeros((8, BLOCK), F32)
    for g0 in range(0, span, BUNCH):
        lows = [(sub * span + (g0 + t)).astype(F32) for t in range(BUNCH)]
        highs = [x + 1.0 for x in lows]

        def some(k, carry):
            olds = list(carry[:many])
            accs = [list(carry[many * (f + 1) : many * (f + 2)]) for f in range(nf)]
            b = PAD + g0 + d0 + k * RUN
            for h in range(2):
                es = [tile(edge.at[h], b + x) for x in range(BUNCH + RUN - 1)]
                qs = [[tile(cols.at[f, h], b + x) for x in range(BUNCH + RUN - 1)] for f in range(nf)]
                for v in range(RUN):
                    for t in range(BUNCH):
                        i = h * BUNCH + t
                        p = jnp.minimum(jnp.maximum(es[v + t], lows[t]), highs[t])
                        w = p - olds[i]
                        olds[i] = p
                        for f in range(nf):
                            accs[f][i] = accs[f][i] + w * qs[f][v + t]
            return (*olds, *sum(accs, []))

        res = lax.fori_loop(0, n, some, (*lows, *lows) + (zero,) * (nf * many))
        for f in range(nf):
            for i, (h, t) in enumerate(spots):
                back[f, h, pl.ds(g0 + t, 8, stride=span), :] = res[many * (f + 1) + i]
    for f in range(nf):
        for h in range(2):
            out[f, 0, :, h * BLOCK : (h + 1) * BLOCK] = back[f, h]


def edges_kernel(thick, e_ref, lo_ref, n_ref, col):
    quarter = thick.shape[3]
    levels = 4 * quarter
    row = lax.broadcasted_iota(jnp.int32, (levels, levels), 0)
    level = (row & 7) * (levels // 8) + lax.shift_right_logical(row, 3)
    j = lax.broadcasted_iota(jnp.int32, (levels, levels), 1)
    lower = (level >= j).astype(F32)
    at_level = level[:, :BLOCK].astype(F32) + 1.0
    low = jnp.zeros((1, 1), F32)
    high = jnp.zeros((1, 1), F32)
    for h in range(2):
        for s in range(4):
            col[h, s * quarter : (s + 1) * quarter, :] = thick[s, 0, h]
        upper = jnp.dot(lower, col[h], precision=HIGH, preferred_element_type=F32)
        e = upper * (levels / upper[levels - 1 :, :])
        e_ref[0, h] = e
        shift = e - at_level
        low = jnp.minimum(low, jnp.min(jnp.min(shift, axis=0, keepdims=True), axis=1, keepdims=True))
        high = jnp.maximum(high, jnp.max(jnp.max(shift, axis=0, keepdims=True), axis=1, keepdims=True))
    lo = jnp.maximum(-jnp.ceil(high), 1.0 - PAD).astype(jnp.int32)
    hi = jnp.minimum(-jnp.floor(low), PAD - 2.0 * RUN).astype(jnp.int32)
    n = lax.shift_right_logical(hi - lo + RUN, RUN.bit_length() - 1)
    lo_ref[0] = jnp.broadcast_to(lo, (1, BLOCK))
    n_ref[0] = jnp.broadcast_to(n, (1, BLOCK))


def edges(thick):
    _, rows, _, quarter, _ = thick.shape
    levels = 4 * quarter
    bound = jax.ShapeDtypeStruct((rows, 1, BLOCK), jnp.int32)
    bspec = pl.BlockSpec((1, 1, BLOCK), lambda r: (r, 0, 0))
    return pl.pallas_call(
        edges_kernel,
        grid=(rows,),
        in_specs=[pl.BlockSpec((4, 1, 2, quarter, BLOCK), lambda r: (0, r, 0, 0, 0))],
        out_specs=[pl.BlockSpec((1, 2, levels, BLOCK), lambda r: (r, 0, 0, 0)), bspec, bspec],
        out_shape=[jax.ShapeDtypeStruct((rows, 2, levels, BLOCK), F32), bound, bound],
        scratch_shapes=[pltpu.VMEM((2, levels, BLOCK), F32)],
        compiler_params=params(12),
        cost_estimate=COST,
        name="edges",
    )(thick)


def halves(x):
    top = x.astype(jnp.bfloat16)
    return top, (x - top.astype(F32)).astype(jnp.bfloat16)


def heat_kernel(row_of, skip, lo_ref, n_ref, own_ref, day_ref, e_ref, exch, solar, so_far, *rest):
    *pieces, out, heating, shares, edge, cols, back, mats = rest
    pieces = pieces[skip:]
    step = pl.program_id(0)
    r = row_of(step)

    @pl.when(step == 0)
    def _():
        shares[...] = so_far[...]
        both = jnp.concatenate([exch[0], exch[1]], axis=1)
        mats[0], mats[1] = halves(both)

    remap_row(lo_ref[r, 0, 0], n_ref[r, 0, 0], e_ref, pieces, edge, cols, back, out)
    temp = out[0, 0]
    hum = out[1, 0]
    levels, width = temp.shape
    square = hum * hum
    clear = 1.0 / (1.0 + square)
    absorb = square * clear
    top, rest_of = halves(jnp.concatenate([absorb * temp, clear * temp], axis=0))
    heat = jnp.dot(mats[0], rest_of, preferred_element_type=F32) + jnp.dot(mats[1], top, preferred_element_type=F32)
    heat = heat + jnp.dot(mats[0], top, preferred_element_type=F32)
    lane = lax.broadcasted_iota(jnp.int32, (1, width), 1)
    d0 = jnp.full((1, width), day_ref[2 * r], jnp.int32)
    d1 = jnp.full((1, width), day_ref[2 * r + 1], jnp.int32)
    day = jnp.where(lane < BLOCK, d0, d1).astype(F32)
    heat = heat + (day * solar[...]) * clear
    heating[0] = heat
    total = jnp.sum(heat, axis=0, keepdims=True)
    line = lax.broadcasted_iota(jnp.int32, (1, BLOCK), 1)
    acc = shares[...]
    for b in range(2):
        mean = jnp.sum(total[:, b * BLOCK : (b + 1) * BLOCK], axis=1, keepdims=True) * (1.0 / (levels * BLOCK))
        acc = acc + jnp.where(line == own_ref[2 * r + b], mean, 0.0)
    shares[...] = acc


def piece_spec(pieces):
    many, _, _, quarter, _ = pieces[0].shape[-5:]
    shape = (many, 1, 2, quarter, BLOCK)
    if len(pieces) == 1:
        return [pl.BlockSpec((4, *shape), lambda r: (0, 0, r, 0, 0, 0))]
    return [pl.BlockSpec(shape, lambda r: (0, r, 0, 0, 0))] * 4


def row_scratch(levels, half):
    tall = levels + 2 * PAD * 8
    return [
        pltpu.VMEM((2, tall, BLOCK), F32),
        pltpu.VMEM((half, 2, tall, BLOCK), F32),
        pltpu.VMEM((half, 2, levels, BLOCK), F32),
    ]


def heat(pieces, bounds, e, rows, row_of, owners, day, exchange, solar, shares, made=()):
    half, count, _, quarter, _ = pieces[0].shape[-5:]
    levels = 4 * quarter
    width = 2 * BLOCK
    whole = pl.BlockSpec((1, BLOCK), lambda r: (0, 0))
    return pl.pallas_call(
        functools.partial(heat_kernel, row_of, len(made)),
        grid=(count,),
        in_specs=[
            SMEM,
            SMEM,
            SMEM,
            SMEM,
            pl.BlockSpec((1, 2, levels, BLOCK), lambda r: (row_of(r), 0, 0, 0)),
            pl.BlockSpec((2, levels, levels), lambda r: (0, 0, 0)),
            pl.BlockSpec((levels, 1), lambda r: (0, 0)),
            whole,
        ]
        + [ANY] * len(made)
        + piece_spec(pieces),
        out_specs=[
            pl.BlockSpec((half, 1, levels, width), lambda r: (0, row_of(r), 0, 0)),
            pl.BlockSpec((1, levels, width), lambda r: (row_of(r), 0, 0)),
            whole,
        ],
        out_shape=[
            jax.ShapeDtypeStruct((2 * half, rows, levels, width), F32),
            jax.ShapeDtypeStruct((rows, levels, width), F32),
            jax.ShapeDtypeStruct((1, BLOCK), F32),
        ],
        input_output_aliases={8: 0, 9: 1} if made else {},
        scratch_shapes=row_scratch(levels, half) + [pltpu.VMEM((2, levels, 2 * levels), jnp.bfloat16)],
        compiler_params=params(12),
        cost_estimate=COST,
        name="heat",
    )(*bounds, owners, day, e, exchange, solar, shares, *made, *pieces)


def remap_kernel(lo_ref, n_ref, e_ref, base, *rest):
    *pieces, out, edge, cols, back = rest
    r = pl.program_id(0)
    remap_row(lo_ref[r, 0, 0], n_ref[r, 0, 0], e_ref, pieces, edge, cols, back, out)


def remap(pieces, bounds, e, base):
    half, rows, _, quarter, _ = pieces[0].shape[-5:]
    levels = 4 * quarter
    width = 2 * BLOCK
    return pl.pallas_call(
        remap_kernel,
        grid=(rows,),
        in_specs=[SMEM] * 2 + [pl.BlockSpec((1, 2, levels, BLOCK), lambda r: (r, 0, 0, 0)), ANY] + piece_spec(pieces),
        out_specs=pl.BlockSpec((half, 1, levels, width), lambda r: (1, r, 0, 0)),
        out_shape=jax.ShapeDtypeStruct((2 * half, rows, levels, width), F32),
        input_output_aliases={3: 0},
        scratch_shapes=row_scratch(levels, half),
        compiler_params=params(12),
        cost_estimate=COST,
        name="remap",
    )(*bounds, e, base, *pieces)


def per_device(fields, thickness, courant_lon, courant_lat, exchange, solar_profile, owners, daylight):
    count = lax.axis_size("lat")
    rows = fields.shape[1]
    ends = count - 1
    hbm = lambda xs: [pltpu.with_memory_space_constraint(x, pltpu.HBM) for x in xs]
    turn = lambda s: [(i, (i + s) % 4) for i in range(4)]
    around = lambda ps: hbm(ps[:1]) + [lax.ppermute(p, "lev", turn(s + 1)) for s, p in enumerate(ps[1:])]
    regroup = lambda x: lax.all_to_all(x, "lev", split_axis=0, concat_axis=0, tiled=True)

    fields, thickness, courant_lon, courant_lat = hbm([fields, thickness, courant_lon, courant_lat])
    thick = spread(thickness)
    head, tail, *inside = inner(fields, courant_lon, courant_lat, *hbm([thick]))
    e, *bounds = edges(regroup(thick))
    prev = lax.ppermute(tail, "lat", [(i, i + 1) for i in range(ends)])
    nxt = lax.ppermute(head, "lat", [(i + 1, i) for i in range(ends)])
    inside = around(inside)
    head, tail = hbm([head, tail])
    outside = [regroup(outer(head, tail, fields, courant_lon, courant_lat, prev, nxt, bounds[0]))]
    second = around(advect(1, fields, courant_lon, courant_lat, prev, nxt))

    other = (owners[:, 0], daylight, exchange, solar_profile[:, None])
    shares = jnp.zeros((1, BLOCK), F32)
    remapped, heating, shares = heat(inside, bounds, e, rows, lambda r: r + 1, *other, shares)
    made = (remapped, heating)
    remapped, heating, shares = heat(outside, bounds, e, rows, lambda r: r * (rows - 1), *other, shares, made)
    remapped = remap(second, bounds, e, remapped)
    shares = shares[0, :count].reshape(count, 1, 1)
    owner_heat = jnp.sum(lax.all_to_all(shares, "lat", split_axis=0, concat_axis=0, tiled=True)).reshape(1, 1)
    return (remapped, heating, owner_heat)


def solution(mesh):
    placed = (
        P(None, "lat", "lev", None),
        P("lat", "lev", None),
        P("lat", "lev", None),
        P("lat", "lev", None),
        P(),
        P(),
        P(("lat", "lev"), None),
        P(("lat", "lev")),
    )
    return jax.shard_map(
        per_device,
        mesh=mesh,
        in_specs=placed,
        out_specs=(P(None, "lat", None, "lev"), P("lat", None, "lev"), P("lat", "lev")),
        check_vma=False,
    )
```

```python
import functools

import jax
import jax.numpy as jnp
from jax import lax
from jax.experimental import pallas as pl
from jax.experimental.pallas import tpu as pltpu
from jax.sharding import PartitionSpec as P

F32 = jnp.float32
HIGH = lax.Precision.HIGHEST
ANY = pl.BlockSpec(memory_space=pl.ANY)
SMEM = pl.BlockSpec(memory_space=pltpu.SMEM)
BLOCK = 128
PAD = 56
RUN = 8
BUNCH = 2
EARLY = 0
MIB = 1024 * 1024


COST = pl.CostEstimate(flops=1, bytes_accessed=1, transcendentals=0)


def params(mib):
    return pltpu.CompilerParams(vmem_limit_bytes=mib * MIB)


def coefs(c):
    sq = 0.5 * c * c
    half = 0.5 * c
    return 1.0 - 2.0 * sq, sq - half, sq + half


def lon_step(x, w):
    n = x.shape[-1]
    mid, up, down = w
    return mid * x + up * pltpu.roll(x, n - 1, 1) + down * pltpu.roll(x, 1, 1)


def staged(ins, outs, sems, body):
    def reads(k):
        return [pltpu.make_async_copy(part(k), buf.at[k], sems.at[k, i]) for i, (part, buf) in enumerate(ins)]

    steps = ins[0][1].shape[0]
    for k in range(steps):
        for c in reads(k):
            c.start()

    def step(k, carry):
        for c in reads(k):
            c.wait()
        body(k, [buf.at[k] for _, buf in ins])
        for c in outs(k):
            c.start()
        return carry

    lax.fori_loop(0, steps, step, 0)
    for k in range(steps):
        for c in outs(k):
            c.wait()


def levs_of(k):
    return pl.ds(pl.multiple_of(k * 8, 8), 8)


def fanned(sent, part, sems, k):
    out = []
    for d in range(4):
        for h in range(2):
            at = (2 * d + h) * BLOCK
            dst = sent.at[(d,) + (slice(None),) * (len(sent.shape) - 4) + (h, levs_of(k), slice(None))]
            out.append(pltpu.make_async_copy(part(pl.ds(at, BLOCK)), dst, sems.at[k, d, h]))
    return out


def spread_kernel(thick, sent, buf, in_sems, sems):
    def outs(k):
        return fanned(sent, lambda cols: buf.at[k, :, :, cols], sems, k)

    staged([(lambda k: thick.at[:, levs_of(k), :], buf)], outs, in_sems, lambda k, bufs: None)


def spread(thickness):
    rows, levs, lon = thickness.shape
    steps = levs // 8
    return pl.pallas_call(
        spread_kernel,
        in_specs=[ANY],
        out_specs=ANY,
        out_shape=pltpu.HBM((4, rows, 2, levs, BLOCK), F32),
        scratch_shapes=[
            pltpu.VMEM((steps, rows, 8, lon), F32),
            pltpu.SemaphoreType.DMA((steps, 1)),
            pltpu.SemaphoreType.DMA((steps, 4, 2)),
        ],
        compiler_params=params(8),
        cost_estimate=COST,
        name="spread",
    )(thickness)


def inner_kernel(fields, c_lon, c_lat, after, head, tail, *rest):
    *sent, q_b, p_b, t_b, lon_b, lat_b, keep, ends, in_sems, sems, end_sems = rest
    nf, rows = q_b.shape[1], q_b.shape[2]
    more = p_b.shape[2]
    ins = [
        (lambda k: fields.at[:nf, :, levs_of(k), :], q_b),
        (lambda k: c_lon.at[:, levs_of(k), :], lon_b),
        (lambda k: fields.at[nf:, :more, levs_of(k), :], p_b),
        (lambda k: fields.at[nf:, rows - 1, levs_of(k), :], t_b),
        (lambda k: c_lat.at[:, levs_of(k), :], lat_b),
    ]

    def outs(k):
        out = turned(sent, lambda cols: keep.at[k, :, :, :, cols], sems, k)
        for e, dst in enumerate((head, tail)):
            out.append(pltpu.make_async_copy(ends.at[k, e], dst.at[:, levs_of(k), :], end_sems.at[k, e]))
        return out

    def body(k, got):
        q, lon, p, tail_in, lat = got
        before = here = None
        for r in range(rows):
            w = coefs(lon[r])
            ahead = [lon_step(q[f, r], w) for f in range(nf)]
            ahead += [lon_step(p[f, r], w) for f in range(nf if r < more else 0)]
            if r == 0:
                for f in range(2 * nf):
                    ends[k, 0, f] = ahead[f]
            if r == rows - 1:
                for f in range(nf):
                    ends[k, 1, f] = ahead[f]
                    ends[k, 1, nf + f] = lon_step(tail_in[f], w)
            if r > 1:
                mid, up, down = coefs(lat[r - 1])
                for f in range(len(ahead)):
                    slot = r - 2 if f < nf else rows - 4 + r
                    keep[k, f % nf, slot] = mid * here[f] + up * ahead[f] + down * before[f]
            before, here = here, ahead

    staged(ins, outs, in_sems, body)


def inner(fields, c_lon, c_lat, after, early):
    nf, rows, levs, lon = fields.shape
    half = nf // 2
    steps = levs // 8
    count = rows - 2 + early
    side = pltpu.HBM((nf, levs, lon), F32)
    sem = pltpu.SemaphoreType.DMA
    shapes = [(half, rows), (half, early + 2), (half,), (rows,), (rows,), (half, count), (2, nf)]
    return pl.pallas_call(
        inner_kernel,
        in_specs=[ANY] * 4,
        out_specs=[ANY] * 6,
        out_shape=[side, side] + [pltpu.HBM((half, count, 2, levs, BLOCK), F32)] * 4,
        scratch_shapes=[pltpu.VMEM((steps, *x, 8, lon), F32) for x in shapes]
        + [sem((steps, 5)), sem((steps, 4, 2)), sem((steps, 2))],
        compiler_params=params(20),
        cost_estimate=COST,
        name="inner",
    )(fields, c_lon, c_lat, after)


def outer_kernel(fields, c_lon, c_lat, head, tail, prev, nxt, after, sent, *rest):
    *bufs, keep, in_sems, sems = rest
    nf = keep.shape[1]
    rows = c_lon.shape[0]
    reads = (
        lambda k: head.at[:nf, levs_of(k), :],
        lambda k: tail.at[:nf, levs_of(k), :],
        lambda k: prev.at[:nf, levs_of(k), :],
        lambda k: nxt.at[:nf, levs_of(k), :],
        lambda k: fields.at[:nf, 1, levs_of(k), :],
        lambda k: fields.at[:nf, rows - 2, levs_of(k), :],
        lambda k: c_lon.at[1, levs_of(k), :],
        lambda k: c_lon.at[rows - 2, levs_of(k), :],
        lambda k: c_lat.at[0, levs_of(k), :],
        lambda k: c_lat.at[rows - 1, levs_of(k), :],
    )

    def outs(k):
        return fanned(sent, lambda cols: keep.at[k, :, :, :, cols], sems, k)

    def body(k, got):
        top, end, north, south, q_top, q_end, lon, lon_end, lat, lat_end = got
        w = coefs(lon[...])
        mid, up, down = coefs(lat[...])
        for f in range(nf):
            keep[k, f, 0] = mid * top[f] + up * lon_step(q_top[f], w) + down * north[f]
        w = coefs(lon_end[...])
        mid, up, down = coefs(lat_end[...])
        for f in range(nf):
            keep[k, f, 1] = mid * end[f] + up * south[f] + down * lon_step(q_end[f], w)

    staged(list(zip(reads, bufs)), outs, in_sems, body)


def outer(fields, c_lon, c_lat, head, tail, prev, nxt, after):
    nf, rows, levs, lon = fields.shape
    half = nf // 2
    steps = levs // 8
    sem = pltpu.SemaphoreType.DMA
    shapes = [(half,)] * 6 + [()] * 4
    return pl.pallas_call(
        outer_kernel,
        in_specs=[ANY] * 8,
        out_specs=ANY,
        out_shape=pltpu.HBM((4, half, 2, 2, levs, BLOCK), F32),
        scratch_shapes=[pltpu.VMEM((steps, *x, 8, lon), F32) for x in shapes]
        + [pltpu.VMEM((steps, half, 2, 8, lon), F32), sem((steps, len(shapes))), sem((steps, 4, 2))],
        compiler_params=params(20),
        cost_estimate=COST,
        name="outer",
    )(fields, c_lon, c_lat, head, tail, prev, nxt, after)


def turned(sent, part, sems, k):
    out = []
    for s, dst in enumerate(sent):
        for h in range(2):
            at = pl.multiple_of(lax.rem(lax.axis_index("lev") + s, 4) * (2 * BLOCK) + h * BLOCK, BLOCK)
            lev = pl.multiple_of(k * 8, 8)
            out.append(
                pltpu.make_async_copy(part(pl.ds(at, BLOCK)), dst.at[:, :, h, pl.ds(lev, 8), :], sems.at[k, s, h])
            )
    return out


def advect_kernel(fields, c_lon, c_lat, prev, nxt, *rest):
    *sent, q_b, lon_b, lat_b, prev_b, nxt_b, keep, in_sems, sems = rest
    nf, count = keep.shape[1], keep.shape[2]
    rows = c_lon.shape[0]
    early = rows - count
    ins = [
        (lambda k: fields.at[nf:, :, levs_of(k), :], q_b),
        (lambda k: c_lon.at[:, levs_of(k), :], lon_b),
        (lambda k: c_lat.at[:, levs_of(k), :], lat_b),
        (lambda k: prev.at[nf:, levs_of(k), :], prev_b),
        (lambda k: nxt.at[nf:, levs_of(k), :], nxt_b),
    ]

    def outs(k):
        return turned(sent, lambda cols: keep.at[k, :, :, :, cols], sems, k)

    def body(k, got):
        q, lon, lat, north, south = got

        def stepped(r):
            w = coefs(lon[r])
            return [lon_step(q[f, r], w) for f in range(nf)]

        def finish(slot, r, before, here, ahead):
            mid, up, down = coefs(lat[r])
            for f in range(nf):
                keep[k, f, slot] = mid * here[f] + up * ahead[f] + down * before[f]

        here, ahead = stepped(0), stepped(1)
        finish(0, 0, [north[f] for f in range(nf)], here, ahead)
        before, here = (stepped(early), stepped(early + 1)) if early else (here, ahead)
        for r in range(early + 1, rows):
            ahead = stepped(r + 1) if r + 1 < rows else [south[f] for f in range(nf)]
            finish(r - early, r, before, here, ahead)
            before, here = here, ahead

    staged(ins, outs, in_sems, body)


def advect(fields, c_lon, c_lat, prev, nxt, early):
    nf, rows, levs, lon = fields.shape
    half, count = nf // 2, rows - early
    steps = levs // 8
    sem = pltpu.SemaphoreType.DMA
    shapes = [(half, rows), (rows,), (rows,), (half,), (half,), (half, count)]
    return pl.pallas_call(
        advect_kernel,
        in_specs=[ANY] * 5,
        out_specs=[ANY] * 4,
        out_shape=[pltpu.HBM((half, count, 2, levs, BLOCK), F32)] * 4,
        scratch_shapes=[pltpu.VMEM((steps, *x, 8, lon), F32) for x in shapes] + [sem((steps, 5)), sem((steps, 4, 2))],
        compiler_params=params(20),
        cost_estimate=COST,
        name="advect",
    )(fields, c_lon, c_lat, prev, nxt)


def source(pieces, k):
    if len(pieces) == 1:
        return pieces[0].at[k], k
    return pieces[k], lax.rem(lax.axis_index("lev") + 4 - k, 4)


def remap_row(d0, n, e_ref, pieces, edge, cols, back, out):
    nf = cols.shape[0]
    quarter = pieces[0].shape[-2]
    levels = 4 * quarter
    span = levels // 8
    sub = lax.broadcasted_iota(jnp.int32, (8, BLOCK), 0)

    def tile(ref, i):
        return ref[pl.ds(pl.multiple_of(i * 8, 8), 8), :]

    for h in range(2):
        edge[h, pl.ds(PAD * 8, levels), :] = e_ref[0, h]
        for k in range(4):
            src, s = source(pieces, k)
            for m in range(quarter // 8):
                at = (PAD + 8 * (m % 2)) * 8 + m // 2 + s * (quarter // span)
                for f in range(nf):
                    cols[f, h, pl.ds(at, 8, stride=8), :] = src[f, 0, h, 8 * m : 8 * m + 8, :]

    def extend(i0, frm, turn, stop, fill):
        edge_row = sub == stop
        for t in range(RUN):
            i = i0 + t
            at = pl.ds(pl.multiple_of(i * 8, 8), 8)
            for h in range(2):
                edge[h, at, :] = jnp.where(edge_row, fill, pltpu.roll(tile(edge.at[h], i + frm), turn, 0))
                for f in range(nf):
                    cols[f, h, at, :] = jnp.where(edge_row, 0.0, pltpu.roll(tile(cols.at[f, h], i + frm), turn, 0))

    def above(k, c):
        extend(PAD + span + k * RUN, -span, 7, 7, 4.0 * levels)
        return c

    def below(k, c):
        extend(PAD - (k + 1) * RUN, span, 1, 0, 0.0)
        return c

    most = lax.shift_right_logical(jnp.maximum(d0 + n * RUN - 1, 0) + RUN - 1, RUN.bit_length() - 1)
    least = lax.shift_right_logical(jnp.maximum(-d0, 0) + RUN - 1, RUN.bit_length() - 1)
    lax.fori_loop(0, most, above, 0)
    lax.fori_loop(0, least, below, 0)

    spots = [(h, t) for h in range(2) for t in range(BUNCH)]
    many = len(spots)
    zero = jnp.zeros((8, BLOCK), F32)
    for g0 in range(0, span, BUNCH):
        lows = [(sub * span + (g0 + t)).astype(F32) for t in range(BUNCH)]
        highs = [x + 1.0 for x in lows]

        def some(k, carry):
            olds = list(carry[:many])
            accs = [list(carry[many * (f + 1) : many * (f + 2)]) for f in range(nf)]
            b = PAD + g0 + d0 + k * RUN
            for h in range(2):
                es = [tile(edge.at[h], b + x) for x in range(BUNCH + RUN - 1)]
                qs = [[tile(cols.at[f, h], b + x) for x in range(BUNCH + RUN - 1)] for f in range(nf)]
                for v in range(RUN):
                    for t in range(BUNCH):
                        i = h * BUNCH + t
                        p = jnp.minimum(jnp.maximum(es[v + t], lows[t]), highs[t])
                        w = p - olds[i]
                        olds[i] = p
                        for f in range(nf):
                            accs[f][i] = accs[f][i] + w * qs[f][v + t]
            return (*olds, *sum(accs, []))

        res = lax.fori_loop(0, n, some, (*lows, *lows) + (zero,) * (nf * many))
        for f in range(nf):
            for i, (h, t) in enumerate(spots):
                back[f, h, pl.ds(g0 + t, 8, stride=span), :] = res[many * (f + 1) + i]
    for f in range(nf):
        for h in range(2):
            out[f, 0, :, h * BLOCK : (h + 1) * BLOCK] = back[f, h]


def edges_kernel(thick, e_ref, lo_ref, n_ref, col):
    quarter = thick.shape[3]
    levels = 4 * quarter
    row = lax.broadcasted_iota(jnp.int32, (levels, levels), 0)
    level = (row & 7) * (levels // 8) + lax.shift_right_logical(row, 3)
    j = lax.broadcasted_iota(jnp.int32, (levels, levels), 1)
    lower = (level >= j).astype(jnp.bfloat16)
    at_level = (level[:, :1] + 1).astype(F32)
    for h in range(2):
        for s in range(4):
            col[s * quarter : (s + 1) * quarter, h * BLOCK : (h + 1) * BLOCK] = thick[s, 0, h]
    top, low = halves(col[...])
    least = col[...] - top.astype(F32) - low.astype(F32)
    upper = jnp.dot(lower, least.astype(jnp.bfloat16), preferred_element_type=F32)
    upper = upper + jnp.dot(lower, low, preferred_element_type=F32)
    upper = upper + jnp.dot(lower, top, preferred_element_type=F32)
    e = upper * (levels / upper[levels - 1 :, :])
    for h in range(2):
        e_ref[0, h] = e[:, h * BLOCK : (h + 1) * BLOCK]
    shift = e - at_level
    low = jnp.minimum(jnp.min(jnp.min(shift, axis=0, keepdims=True), axis=1, keepdims=True), 0.0)
    high = jnp.maximum(jnp.max(jnp.max(shift, axis=0, keepdims=True), axis=1, keepdims=True), 0.0)
    lo = jnp.maximum(-jnp.ceil(high), 1.0 - PAD).astype(jnp.int32)
    hi = jnp.minimum(-jnp.floor(low), PAD - 2.0 * RUN).astype(jnp.int32)
    n = lax.shift_right_logical(hi - lo + RUN, RUN.bit_length() - 1)
    lo_ref[0] = jnp.broadcast_to(lo, (1, BLOCK))
    n_ref[0] = jnp.broadcast_to(n, (1, BLOCK))


def edges(thick):
    _, rows, _, quarter, _ = thick.shape
    levels = 4 * quarter
    bound = jax.ShapeDtypeStruct((rows, 1, BLOCK), jnp.int32)
    bspec = pl.BlockSpec((1, 1, BLOCK), lambda r: (r, 0, 0))
    return pl.pallas_call(
        edges_kernel,
        grid=(rows,),
        in_specs=[pl.BlockSpec((4, 1, 2, quarter, BLOCK), lambda r: (0, r, 0, 0, 0))],
        out_specs=[pl.BlockSpec((1, 2, levels, BLOCK), lambda r: (r, 0, 0, 0)), bspec, bspec],
        out_shape=[jax.ShapeDtypeStruct((rows, 2, levels, BLOCK), F32), bound, bound],
        scratch_shapes=[pltpu.VMEM((levels, 2 * BLOCK), F32)],
        compiler_params=params(12),
        cost_estimate=COST,
        name="edges",
    )(thick)


def halves(x):
    top = x.astype(jnp.bfloat16)
    return top, (x - top.astype(F32)).astype(jnp.bfloat16)


def heat_kernel(row_of, skip, lo_ref, n_ref, own_ref, day_ref, e_ref, exch, solar, so_far, *rest):
    *pieces, out, heating, shares, edge, cols, back, mats = rest
    pieces = pieces[skip:]
    step = pl.program_id(0)
    r = row_of(step)

    @pl.when(step == 0)
    def _():
        shares[...] = so_far[...]
        both = jnp.concatenate([exch[0], exch[1]], axis=1)
        mats[0], mats[1] = halves(both)

    remap_row(lo_ref[r, 0, 0], n_ref[r, 0, 0], e_ref, pieces, edge, cols, back, out)
    temp = out[0, 0]
    hum = out[1, 0]
    levels, width = temp.shape
    square = hum * hum
    clear = 1.0 / (1.0 + square)
    absorb = square * clear
    top, rest_of = halves(jnp.concatenate([absorb * temp, clear * temp], axis=0))
    heat = jnp.dot(mats[0], rest_of, preferred_element_type=F32) + jnp.dot(mats[1], top, preferred_element_type=F32)
    heat = heat + jnp.dot(mats[0], top, preferred_element_type=F32)
    lane = lax.broadcasted_iota(jnp.int32, (1, width), 1)
    d0 = jnp.full((1, width), day_ref[2 * r], jnp.int32)
    d1 = jnp.full((1, width), day_ref[2 * r + 1], jnp.int32)
    day = jnp.where(lane < BLOCK, d0, d1).astype(F32)
    heat = heat + (day * solar[...]) * clear
    heating[0] = heat
    total = jnp.sum(heat, axis=0, keepdims=True)
    line = lax.broadcasted_iota(jnp.int32, (1, BLOCK), 1)
    acc = shares[...]
    for b in range(2):
        mean = jnp.sum(total[:, b * BLOCK : (b + 1) * BLOCK], axis=1, keepdims=True) * (1.0 / (levels * BLOCK))
        acc = acc + jnp.where(line == own_ref[2 * r + b], mean, 0.0)
    shares[...] = acc


def piece_spec(pieces, skip=0):
    many, _, _, quarter, _ = pieces[0].shape[-5:]
    shape = (many, 1, 2, quarter, BLOCK)
    if len(pieces) == 1:
        return [pl.BlockSpec((4, *shape), lambda r: (0, 0, skip + r, 0, 0, 0))]
    return [pl.BlockSpec(shape, lambda r: (0, skip + r, 0, 0, 0))] * 4


def row_scratch(levels, half):
    tall = levels + 2 * PAD * 8
    return [
        pltpu.VMEM((2, tall, BLOCK), F32),
        pltpu.VMEM((half, 2, tall, BLOCK), F32),
        pltpu.VMEM((half, 2, levels, BLOCK), F32),
    ]


def heat(pieces, count, bounds, e, rows, row_of, owners, day, exchange, solar, shares, made=()):
    half, _, _, quarter, _ = pieces[0].shape[-5:]
    levels = 4 * quarter
    width = 2 * BLOCK
    whole = pl.BlockSpec((1, BLOCK), lambda r: (0, 0))
    return pl.pallas_call(
        functools.partial(heat_kernel, row_of, len(made)),
        grid=(count,),
        in_specs=[
            SMEM,
            SMEM,
            SMEM,
            SMEM,
            pl.BlockSpec((1, 2, levels, BLOCK), lambda r: (row_of(r), 0, 0, 0)),
            pl.BlockSpec((2, levels, levels), lambda r: (0, 0, 0)),
            pl.BlockSpec((levels, 1), lambda r: (0, 0)),
            whole,
        ]
        + [ANY] * len(made)
        + piece_spec(pieces),
        out_specs=[
            pl.BlockSpec((half, 1, levels, width), lambda r: (0, row_of(r), 0, 0)),
            pl.BlockSpec((1, levels, width), lambda r: (row_of(r), 0, 0)),
            whole,
        ],
        out_shape=[
            jax.ShapeDtypeStruct((2 * half, rows, levels, width), F32),
            jax.ShapeDtypeStruct((rows, levels, width), F32),
            jax.ShapeDtypeStruct((1, BLOCK), F32),
        ],
        input_output_aliases={8: 0, 9: 1} if made else {},
        scratch_shapes=row_scratch(levels, half) + [pltpu.VMEM((2, levels, 2 * levels), jnp.bfloat16)],
        compiler_params=params(12),
        cost_estimate=COST,
        name="heat",
    )(*bounds, owners, day, e, exchange, solar, shares, *made, *pieces)


def remap_kernel(row_of, lo_ref, n_ref, e_ref, base, *rest):
    *pieces, out, edge, cols, back = rest
    r = row_of(pl.program_id(0))
    remap_row(lo_ref[r, 0, 0], n_ref[r, 0, 0], e_ref, pieces, edge, cols, back, out)


def remap(pieces, skip, count, row_of, bounds, e, base):
    half, _, _, quarter, _ = pieces[0].shape[-5:]
    levels = 4 * quarter
    width = 2 * BLOCK
    return pl.pallas_call(
        functools.partial(remap_kernel, row_of),
        grid=(count,),
        in_specs=[SMEM] * 2
        + [pl.BlockSpec((1, 2, levels, BLOCK), lambda r: (row_of(r), 0, 0, 0)), ANY]
        + piece_spec(pieces, skip),
        out_specs=pl.BlockSpec((half, 1, levels, width), lambda r: (1, row_of(r), 0, 0)),
        out_shape=jax.ShapeDtypeStruct(base.shape, F32),
        input_output_aliases={3: 0},
        scratch_shapes=row_scratch(levels, half),
        compiler_params=params(12),
        cost_estimate=COST,
        name="remap",
    )(*bounds, e, base, *pieces)


def per_device(fields, thickness, courant_lon, courant_lat, exchange, solar_profile, owners, daylight):
    count = lax.axis_size("lat")
    rows = fields.shape[1]
    ends = count - 1
    hbm = lambda xs: [pltpu.with_memory_space_constraint(x, pltpu.HBM) for x in xs]
    turn = lambda s: [(i, (i + s) % 4) for i in range(4)]
    around = lambda ps: hbm(ps[:1]) + [lax.ppermute(p, "lev", turn(s + 1)) for s, p in enumerate(ps[1:])]
    regroup = lambda x: lax.all_to_all(x, "lev", split_axis=0, concat_axis=0, tiled=True)

    fields, thickness, courant_lon, courant_lat = hbm([fields, thickness, courant_lon, courant_lat])
    thick = spread(thickness)
    head, tail, *inside = inner(fields, courant_lon, courant_lat, *hbm([thick]), EARLY)
    e, *bounds = edges(regroup(thick))
    prev = lax.ppermute(tail, "lat", [(i, i + 1) for i in range(ends)])
    nxt = lax.ppermute(head, "lat", [(i + 1, i) for i in range(ends)])
    inside = around(inside)
    head, tail = hbm([head, tail])
    outside = [regroup(outer(fields, courant_lon, courant_lat, head, tail, prev, nxt, bounds[0]))]
    second = around(advect(fields, courant_lon, courant_lat, prev, nxt, EARLY))

    other = (owners[:, 0], daylight, exchange, solar_profile[:, None])
    shares = jnp.zeros((1, BLOCK), F32)
    remapped, heating, shares = heat(inside, rows - 2, bounds, e, rows, lambda r: r + 1, *other, shares)
    made = (remapped, heating)
    remapped, heating, shares = heat(outside, 2, bounds, e, rows, lambda r: r * (rows - 1), *other, shares, made)
    later = lambda r: r + EARLY * jnp.minimum(r, 1)
    remapped = remap(second, 0, rows - EARLY, later, bounds, e, remapped)
    shares = shares[0, :count].reshape(count, 1, 1)
    owner_heat = jnp.sum(lax.all_to_all(shares, "lat", split_axis=0, concat_axis=0, tiled=True)).reshape(1, 1)
    return (remapped, heating, owner_heat)


def solution(mesh):
    placed = (
        P(None, "lat", "lev", None),
        P("lat", "lev", None),
        P("lat", "lev", None),
        P("lat", "lev", None),
        P(),
        P(),
        P(("lat", "lev"), None),
        P(("lat", "lev")),
    )
    return jax.shard_map(
        per_device,
        mesh=mesh,
        in_specs=placed,
        out_specs=(P(None, "lat", None, "lev"), P("lat", None, "lev"), P("lat", "lev")),
        check_vma=False,
    )
```

```python
import functools

import jax
import jax.numpy as jnp
from jax import lax
from jax.experimental import pallas as pl
from jax.experimental.pallas import tpu as pltpu
from jax.sharding import PartitionSpec as P

F32 = jnp.float32
HIGH = lax.Precision.HIGHEST
ANY = pl.BlockSpec(memory_space=pl.ANY)
SMEM = pl.BlockSpec(memory_space=pltpu.SMEM)
BLOCK = 128
PAD = 56
RUN = 8
BUNCH = 2
EARLY = 0
MIB = 1024 * 1024


COST = pl.CostEstimate(flops=1, bytes_accessed=1, transcendentals=0)


def params(mib):
    return pltpu.CompilerParams(vmem_limit_bytes=mib * MIB)


def coefs(c):
    sq = 0.5 * c * c
    half = 0.5 * c
    return 1.0 - 2.0 * sq, sq - half, sq + half


def lon_step(x, w):
    n = x.shape[-1]
    mid, up, down = w
    return mid * x + up * pltpu.roll(x, n - 1, 1) + down * pltpu.roll(x, 1, 1)


def staged(ins, outs, sems, body):
    def reads(k):
        return [pltpu.make_async_copy(part(k), buf.at[k], sems.at[k, i]) for i, (part, buf) in enumerate(ins)]

    steps = ins[0][1].shape[0]
    for k in range(steps):
        for c in reads(k):
            c.start()

    def step(k, carry):
        for c in reads(k):
            c.wait()
        body(k, [buf.at[k] for _, buf in ins])
        for c in outs(k):
            c.start()
        return carry

    lax.fori_loop(0, steps, step, 0)
    for k in range(steps):
        for c in outs(k):
            c.wait()


def levs_of(k):
    return pl.ds(pl.multiple_of(k * 8, 8), 8)


def fanned(sent, part, sems, k):
    out = []
    for d in range(4):
        for h in range(2):
            at = (2 * d + h) * BLOCK
            dst = sent.at[(d,) + (slice(None),) * (len(sent.shape) - 4) + (h, levs_of(k), slice(None))]
            out.append(pltpu.make_async_copy(part(pl.ds(at, BLOCK)), dst, sems.at[k, d, h]))
    return out


def spread_kernel(thick, sent, buf, in_sems, sems):
    def outs(k):
        return fanned(sent, lambda cols: buf.at[k, :, :, cols], sems, k)

    staged([(lambda k: thick.at[:, levs_of(k), :], buf)], outs, in_sems, lambda k, bufs: None)


def spread(thickness):
    rows, levs, lon = thickness.shape
    steps = levs // 8
    return pl.pallas_call(
        spread_kernel,
        in_specs=[ANY],
        out_specs=ANY,
        out_shape=pltpu.HBM((4, rows, 2, levs, BLOCK), F32),
        scratch_shapes=[
            pltpu.VMEM((steps, rows, 8, lon), F32),
            pltpu.SemaphoreType.DMA((steps, 1)),
            pltpu.SemaphoreType.DMA((steps, 4, 2)),
        ],
        compiler_params=params(8),
        cost_estimate=COST,
        name="spread",
    )(thickness)


def inner_kernel(fields, c_lon, c_lat, after, head, tail, *rest):
    *sent, q_b, p_b, t_b, lon_b, lat_b, keep, ends, in_sems, sems, end_sems = rest
    nf, rows = q_b.shape[1], q_b.shape[2]
    more = p_b.shape[2]
    ins = [
        (lambda k: fields.at[:nf, :, levs_of(k), :], q_b),
        (lambda k: c_lon.at[:, levs_of(k), :], lon_b),
        (lambda k: fields.at[nf:, :more, levs_of(k), :], p_b),
        (lambda k: fields.at[nf:, rows - 1, levs_of(k), :], t_b),
        (lambda k: c_lat.at[:, levs_of(k), :], lat_b),
    ]

    def outs(k):
        out = turned(sent, lambda cols: keep.at[k, :, :, :, cols], sems, k)
        for e, dst in enumerate((head, tail)):
            out.append(pltpu.make_async_copy(ends.at[k, e], dst.at[:, levs_of(k), :], end_sems.at[k, e]))
        return out

    def body(k, got):
        q, lon, p, tail_in, lat = got
        before = here = None
        for r in range(rows):
            w = coefs(lon[r])
            ahead = [lon_step(q[f, r], w) for f in range(nf)]
            ahead += [lon_step(p[f, r], w) for f in range(nf if r < more else 0)]
            if r == 0:
                for f in range(2 * nf):
                    ends[k, 0, f] = ahead[f]
            if r == rows - 1:
                for f in range(nf):
                    ends[k, 1, f] = ahead[f]
                    ends[k, 1, nf + f] = lon_step(tail_in[f], w)
            if r > 1:
                mid, up, down = coefs(lat[r - 1])
                for f in range(len(ahead)):
                    slot = r - 2 if f < nf else rows - 4 + r
                    keep[k, f % nf, slot] = mid * here[f] + up * ahead[f] + down * before[f]
            before, here = here, ahead

    staged(ins, outs, in_sems, body)


def inner(fields, c_lon, c_lat, after, early):
    nf, rows, levs, lon = fields.shape
    half = nf // 2
    steps = levs // 8
    count = rows - 2 + early
    side = pltpu.HBM((nf, levs, lon), F32)
    sem = pltpu.SemaphoreType.DMA
    shapes = [(half, rows), (half, early + 2), (half,), (rows,), (rows,), (half, count), (2, nf)]
    return pl.pallas_call(
        inner_kernel,
        in_specs=[ANY] * 4,
        out_specs=[ANY] * 6,
        out_shape=[side, side] + [pltpu.HBM((half, count, 2, levs, BLOCK), F32)] * 4,
        scratch_shapes=[pltpu.VMEM((steps, *x, 8, lon), F32) for x in shapes]
        + [sem((steps, 5)), sem((steps, 4, 2)), sem((steps, 2))],
        compiler_params=params(20),
        cost_estimate=COST,
        name="inner",
    )(fields, c_lon, c_lat, after)


def outer_kernel(fields, c_lon, c_lat, head, tail, prev, nxt, after, sent, *rest):
    *bufs, keep, in_sems, sems = rest
    nf = keep.shape[1]
    rows = c_lon.shape[0]
    reads = (
        lambda k: head.at[:nf, levs_of(k), :],
        lambda k: tail.at[:nf, levs_of(k), :],
        lambda k: prev.at[:nf, levs_of(k), :],
        lambda k: nxt.at[:nf, levs_of(k), :],
        lambda k: fields.at[:nf, 1, levs_of(k), :],
        lambda k: fields.at[:nf, rows - 2, levs_of(k), :],
        lambda k: c_lon.at[1, levs_of(k), :],
        lambda k: c_lon.at[rows - 2, levs_of(k), :],
        lambda k: c_lat.at[0, levs_of(k), :],
        lambda k: c_lat.at[rows - 1, levs_of(k), :],
    )

    def outs(k):
        return fanned(sent, lambda cols: keep.at[k, :, :, :, cols], sems, k)

    def body(k, got):
        top, end, north, south, q_top, q_end, lon, lon_end, lat, lat_end = got
        w = coefs(lon[...])
        mid, up, down = coefs(lat[...])
        for f in range(nf):
            keep[k, f, 0] = mid * top[f] + up * lon_step(q_top[f], w) + down * north[f]
        w = coefs(lon_end[...])
        mid, up, down = coefs(lat_end[...])
        for f in range(nf):
            keep[k, f, 1] = mid * end[f] + up * south[f] + down * lon_step(q_end[f], w)

    staged(list(zip(reads, bufs)), outs, in_sems, body)


def outer(fields, c_lon, c_lat, head, tail, prev, nxt, after):
    nf, rows, levs, lon = fields.shape
    half = nf // 2
    steps = levs // 8
    sem = pltpu.SemaphoreType.DMA
    shapes = [(half,)] * 6 + [()] * 4
    return pl.pallas_call(
        outer_kernel,
        in_specs=[ANY] * 8,
        out_specs=ANY,
        out_shape=pltpu.HBM((4, half, 2, 2, levs, BLOCK), F32),
        scratch_shapes=[pltpu.VMEM((steps, *x, 8, lon), F32) for x in shapes]
        + [pltpu.VMEM((steps, half, 2, 8, lon), F32), sem((steps, len(shapes))), sem((steps, 4, 2))],
        compiler_params=params(20),
        cost_estimate=COST,
        name="outer",
    )(fields, c_lon, c_lat, head, tail, prev, nxt, after)


def turned(sent, part, sems, k):
    out = []
    for s, dst in enumerate(sent):
        for h in range(2):
            at = pl.multiple_of(lax.rem(lax.axis_index("lev") + s, 4) * (2 * BLOCK) + h * BLOCK, BLOCK)
            lev = pl.multiple_of(k * 8, 8)
            out.append(
                pltpu.make_async_copy(part(pl.ds(at, BLOCK)), dst.at[:, :, h, pl.ds(lev, 8), :], sems.at[k, s, h])
            )
    return out


def advect_kernel(fields, c_lon, c_lat, prev, nxt, *rest):
    *sent, q_b, lon_b, lat_b, prev_b, nxt_b, keep, in_sems, sems = rest
    nf, count = keep.shape[1], keep.shape[2]
    rows = c_lon.shape[0]
    early = rows - count
    ins = [
        (lambda k: fields.at[nf:, :, levs_of(k), :], q_b),
        (lambda k: c_lon.at[:, levs_of(k), :], lon_b),
        (lambda k: c_lat.at[:, levs_of(k), :], lat_b),
        (lambda k: prev.at[nf:, levs_of(k), :], prev_b),
        (lambda k: nxt.at[nf:, levs_of(k), :], nxt_b),
    ]

    def outs(k):
        return turned(sent, lambda cols: keep.at[k, :, :, :, cols], sems, k)

    def body(k, got):
        q, lon, lat, north, south = got

        def stepped(r):
            w = coefs(lon[r])
            return [lon_step(q[f, r], w) for f in range(nf)]

        def finish(slot, r, before, here, ahead):
            mid, up, down = coefs(lat[r])
            for f in range(nf):
                keep[k, f, slot] = mid * here[f] + up * ahead[f] + down * before[f]

        here, ahead = stepped(0), stepped(1)
        finish(0, 0, [north[f] for f in range(nf)], here, ahead)
        before, here = (stepped(early), stepped(early + 1)) if early else (here, ahead)
        for r in range(early + 1, rows):
            ahead = stepped(r + 1) if r + 1 < rows else [south[f] for f in range(nf)]
            finish(r - early, r, before, here, ahead)
            before, here = here, ahead

    staged(ins, outs, in_sems, body)


def advect(fields, c_lon, c_lat, prev, nxt, early):
    nf, rows, levs, lon = fields.shape
    half, count = nf // 2, rows - early
    steps = levs // 8
    sem = pltpu.SemaphoreType.DMA
    shapes = [(half, rows), (rows,), (rows,), (half,), (half,), (half, count)]
    return pl.pallas_call(
        advect_kernel,
        in_specs=[ANY] * 5,
        out_specs=[ANY] * 4,
        out_shape=[pltpu.HBM((half, count, 2, levs, BLOCK), F32)] * 4,
        scratch_shapes=[pltpu.VMEM((steps, *x, 8, lon), F32) for x in shapes] + [sem((steps, 5)), sem((steps, 4, 2))],
        compiler_params=params(20),
        cost_estimate=COST,
        name="advect",
    )(fields, c_lon, c_lat, prev, nxt)


def source(pieces, k):
    if len(pieces) == 1:
        return pieces[0].at[k], k
    return pieces[k], lax.rem(lax.axis_index("lev") + 4 - k, 4)


def remap_row(d0, n, e_ref, pieces, edge, cols, back, out):
    nf = cols.shape[0]
    quarter = pieces[0].shape[-2]
    levels = 4 * quarter
    span = levels // 8
    sub = lax.broadcasted_iota(jnp.int32, (8, BLOCK), 0)

    def tile(ref, i):
        return ref[pl.ds(pl.multiple_of(i * 8, 8), 8), :]

    for h in range(2):
        edge[h, pl.ds(PAD * 8, levels), :] = e_ref[0, h]
        for k in range(4):
            src, s = source(pieces, k)
            for m in range(quarter // 8):
                at = (PAD + 8 * (m % 2)) * 8 + m // 2 + s * (quarter // span)
                for f in range(nf):
                    cols[f, h, pl.ds(at, 8, stride=8), :] = src[f, 0, h, 8 * m : 8 * m + 8, :]

    def extend(i0, frm, turn, stop, fill):
        edge_row = sub == stop
        for t in range(RUN):
            i = i0 + t
            at = pl.ds(pl.multiple_of(i * 8, 8), 8)
            for h in range(2):
                edge[h, at, :] = jnp.where(edge_row, fill, pltpu.roll(tile(edge.at[h], i + frm), turn, 0))
                for f in range(nf):
                    cols[f, h, at, :] = jnp.where(edge_row, 0.0, pltpu.roll(tile(cols.at[f, h], i + frm), turn, 0))

    def above(k, c):
        extend(PAD + span + k * RUN, -span, 7, 7, 4.0 * levels)
        return c

    def below(k, c):
        extend(PAD - (k + 1) * RUN, span, 1, 0, 0.0)
        return c

    most = lax.shift_right_logical(jnp.maximum(d0 + n * RUN - 1, 0) + RUN - 1, RUN.bit_length() - 1)
    least = lax.shift_right_logical(jnp.maximum(-d0, 0) + RUN - 1, RUN.bit_length() - 1)
    lax.fori_loop(0, most, above, 0)
    lax.fori_loop(0, least, below, 0)

    spots = [(h, t) for h in range(2) for t in range(BUNCH)]
    many = len(spots)
    zero = jnp.zeros((8, BLOCK), F32)
    for g0 in range(0, span, BUNCH):
        lows = [(sub * span + (g0 + t)).astype(F32) for t in range(BUNCH)]
        highs = [x + 1.0 for x in lows]

        def some(k, carry):
            olds = list(carry[:many])
            accs = [list(carry[many * (f + 1) : many * (f + 2)]) for f in range(nf)]
            b = PAD + g0 + d0 + k * RUN
            for h in range(2):
                es = [tile(edge.at[h], b + x) for x in range(BUNCH + RUN - 1)]
                qs = [[tile(cols.at[f, h], b + x) for x in range(BUNCH + RUN - 1)] for f in range(nf)]
                for v in range(RUN):
                    for t in range(BUNCH):
                        i = h * BUNCH + t
                        p = jnp.minimum(jnp.maximum(es[v + t], lows[t]), highs[t])
                        w = p - olds[i]
                        olds[i] = p
                        for f in range(nf):
                            accs[f][i] = accs[f][i] + w * qs[f][v + t]
            return (*olds, *sum(accs, []))

        res = lax.fori_loop(0, n, some, (*lows, *lows) + (zero,) * (nf * many))
        for f in range(nf):
            for i, (h, t) in enumerate(spots):
                back[f, h, pl.ds(g0 + t, 8, stride=span), :] = res[many * (f + 1) + i]
    for f in range(nf):
        for h in range(2):
            out[f, 0, :, h * BLOCK : (h + 1) * BLOCK] = back[f, h]


def edges_kernel(thick, e_ref, lo_ref, n_ref, col):
    quarter = thick.shape[3]
    levels = 4 * quarter
    row = lax.broadcasted_iota(jnp.int32, (levels, levels), 0)
    level = (row & 7) * (levels // 8) + lax.shift_right_logical(row, 3)
    j = lax.broadcasted_iota(jnp.int32, (levels, levels), 1)
    lower = (level >= j).astype(jnp.bfloat16)
    at_level = (level[:, :1] + 1).astype(F32)
    for h in range(2):
        for s in range(4):
            col[s * quarter : (s + 1) * quarter, h * BLOCK : (h + 1) * BLOCK] = thick[s, 0, h]
    top, low = halves(col[...])
    least = col[...] - top.astype(F32) - low.astype(F32)
    upper = jnp.dot(lower, least.astype(jnp.bfloat16), preferred_element_type=F32)
    upper = upper + jnp.dot(lower, low, preferred_element_type=F32)
    upper = upper + jnp.dot(lower, top, preferred_element_type=F32)
    e = upper * (levels / upper[levels - 1 :, :])
    for h in range(2):
        e_ref[0, h] = e[:, h * BLOCK : (h + 1) * BLOCK]
    shift = e - at_level
    low = jnp.minimum(jnp.min(jnp.min(shift, axis=0, keepdims=True), axis=1, keepdims=True), 0.0)
    high = jnp.maximum(jnp.max(jnp.max(shift, axis=0, keepdims=True), axis=1, keepdims=True), 0.0)
    lo = jnp.maximum(-jnp.ceil(high), 1.0 - PAD).astype(jnp.int32)
    hi = jnp.minimum(-jnp.floor(low), PAD - 2.0 * RUN).astype(jnp.int32)
    n = lax.shift_right_logical(hi - lo + RUN, RUN.bit_length() - 1)
    lo_ref[0] = jnp.broadcast_to(lo, (1, BLOCK))
    n_ref[0] = jnp.broadcast_to(n, (1, BLOCK))


def edges(thick):
    _, rows, _, quarter, _ = thick.shape
    levels = 4 * quarter
    bound = jax.ShapeDtypeStruct((rows, 1, BLOCK), jnp.int32)
    bspec = pl.BlockSpec((1, 1, BLOCK), lambda r: (r, 0, 0))
    return pl.pallas_call(
        edges_kernel,
        grid=(rows,),
        in_specs=[pl.BlockSpec((4, 1, 2, quarter, BLOCK), lambda r: (0, r, 0, 0, 0))],
        out_specs=[pl.BlockSpec((1, 2, levels, BLOCK), lambda r: (r, 0, 0, 0)), bspec, bspec],
        out_shape=[jax.ShapeDtypeStruct((rows, 2, levels, BLOCK), F32), bound, bound],
        scratch_shapes=[pltpu.VMEM((levels, 2 * BLOCK), F32)],
        compiler_params=params(12),
        cost_estimate=COST,
        name="edges",
    )(thick)


def halves(x):
    top = x.astype(jnp.bfloat16)
    return top, (x - top.astype(F32)).astype(jnp.bfloat16)


def heat_kernel(row_of, skip, lo_ref, n_ref, own_ref, day_ref, e_ref, exch, solar, so_far, *rest):
    *pieces, out, heating, shares, edge, cols, back, mats = rest
    pieces = pieces[skip:]
    step = pl.program_id(0)
    r = row_of(step)

    @pl.when(step == 0)
    def _():
        shares[...] = so_far[...]
        both = jnp.concatenate([exch[0], exch[1]], axis=1)
        mats[0], mats[1] = halves(both)

    remap_row(lo_ref[r, 0, 0], n_ref[r, 0, 0], e_ref, pieces, edge, cols, back, out)
    temp = out[0, 0]
    hum = out[1, 0]
    levels, width = temp.shape
    square = hum * hum
    clear = 1.0 / (1.0 + square)
    absorb = square * clear
    top, rest_of = halves(jnp.concatenate([absorb * temp, clear * temp], axis=0))
    heat = jnp.dot(mats[0], rest_of, preferred_element_type=F32) + jnp.dot(mats[1], top, preferred_element_type=F32)
    heat = heat + jnp.dot(mats[0], top, preferred_element_type=F32)
    lane = lax.broadcasted_iota(jnp.int32, (1, width), 1)
    d0 = jnp.full((1, width), day_ref[2 * r], jnp.int32)
    d1 = jnp.full((1, width), day_ref[2 * r + 1], jnp.int32)
    day = jnp.where(lane < BLOCK, d0, d1).astype(F32)
    heat = heat + (day * solar[...]) * clear
    heating[0] = heat
    total = jnp.sum(heat, axis=0, keepdims=True)
    for b in range(2):
        own = own_ref[2 * r + b]
        shares[own] = shares[own] + total[:, b * BLOCK : (b + 1) * BLOCK] * (1.0 / (levels * BLOCK))


def piece_spec(pieces, skip=0):
    many, _, _, quarter, _ = pieces[0].shape[-5:]
    shape = (many, 1, 2, quarter, BLOCK)
    if len(pieces) == 1:
        return [pl.BlockSpec((4, *shape), lambda r: (0, 0, skip + r, 0, 0, 0))]
    return [pl.BlockSpec(shape, lambda r: (0, skip + r, 0, 0, 0))] * 4


def row_scratch(levels, half):
    tall = levels + 2 * PAD * 8
    return [
        pltpu.VMEM((2, tall, BLOCK), F32),
        pltpu.VMEM((half, 2, tall, BLOCK), F32),
        pltpu.VMEM((half, 2, levels, BLOCK), F32),
    ]


def heat(pieces, count, bounds, e, rows, row_of, owners, day, exchange, solar, shares, made=()):
    half, _, _, quarter, _ = pieces[0].shape[-5:]
    levels = 4 * quarter
    width = 2 * BLOCK
    whole = pl.BlockSpec(shares.shape, lambda r: (0, 0, 0))
    return pl.pallas_call(
        functools.partial(heat_kernel, row_of, len(made)),
        grid=(count,),
        in_specs=[
            SMEM,
            SMEM,
            SMEM,
            SMEM,
            pl.BlockSpec((1, 2, levels, BLOCK), lambda r: (row_of(r), 0, 0, 0)),
            pl.BlockSpec((2, levels, levels), lambda r: (0, 0, 0)),
            pl.BlockSpec((levels, 1), lambda r: (0, 0)),
            whole,
        ]
        + [ANY] * len(made)
        + piece_spec(pieces),
        out_specs=[
            pl.BlockSpec((half, 1, levels, width), lambda r: (0, row_of(r), 0, 0)),
            pl.BlockSpec((1, levels, width), lambda r: (row_of(r), 0, 0)),
            whole,
        ],
        out_shape=[
            jax.ShapeDtypeStruct((2 * half, rows, levels, width), F32),
            jax.ShapeDtypeStruct((rows, levels, width), F32),
            jax.ShapeDtypeStruct(shares.shape, F32),
        ],
        input_output_aliases={8: 0, 9: 1} if made else {},
        scratch_shapes=row_scratch(levels, half) + [pltpu.VMEM((2, levels, 2 * levels), jnp.bfloat16)],
        compiler_params=params(12),
        cost_estimate=COST,
        name="heat",
    )(*bounds, owners, day, e, exchange, solar, shares, *made, *pieces)


def remap_kernel(row_of, lo_ref, n_ref, e_ref, base, *rest):
    *pieces, out, edge, cols, back = rest
    r = row_of(pl.program_id(0))
    remap_row(lo_ref[r, 0, 0], n_ref[r, 0, 0], e_ref, pieces, edge, cols, back, out)


def remap(pieces, skip, count, row_of, bounds, e, base):
    half, _, _, quarter, _ = pieces[0].shape[-5:]
    levels = 4 * quarter
    width = 2 * BLOCK
    return pl.pallas_call(
        functools.partial(remap_kernel, row_of),
        grid=(count,),
        in_specs=[SMEM] * 2
        + [pl.BlockSpec((1, 2, levels, BLOCK), lambda r: (row_of(r), 0, 0, 0)), ANY]
        + piece_spec(pieces, skip),
        out_specs=pl.BlockSpec((half, 1, levels, width), lambda r: (1, row_of(r), 0, 0)),
        out_shape=jax.ShapeDtypeStruct(base.shape, F32),
        input_output_aliases={3: 0},
        scratch_shapes=row_scratch(levels, half),
        compiler_params=params(12),
        cost_estimate=COST,
        name="remap",
    )(*bounds, e, base, *pieces)


def per_device(fields, thickness, courant_lon, courant_lat, exchange, solar_profile, owners, daylight):
    count = lax.axis_size("lat")
    rows = fields.shape[1]
    ends = count - 1
    hbm = lambda xs: [pltpu.with_memory_space_constraint(x, pltpu.HBM) for x in xs]
    turn = lambda s: [(i, (i + s) % 4) for i in range(4)]
    around = lambda ps: hbm(ps[:1]) + [lax.ppermute(p, "lev", turn(s + 1)) for s, p in enumerate(ps[1:])]
    regroup = lambda x: lax.all_to_all(x, "lev", split_axis=0, concat_axis=0, tiled=True)

    fields, thickness, courant_lon, courant_lat = hbm([fields, thickness, courant_lon, courant_lat])
    thick = spread(thickness)
    head, tail, *inside = inner(fields, courant_lon, courant_lat, *hbm([thick]), EARLY)
    e, *bounds = edges(regroup(thick))
    prev = lax.ppermute(tail, "lat", [(i, i + 1) for i in range(ends)])
    nxt = lax.ppermute(head, "lat", [(i + 1, i) for i in range(ends)])
    inside = around(inside)
    head, tail = hbm([head, tail])
    outside = [regroup(outer(fields, courant_lon, courant_lat, head, tail, prev, nxt, bounds[0]))]
    second = around(advect(fields, courant_lon, courant_lat, prev, nxt, EARLY))

    other = (owners[:, 0], daylight, exchange, solar_profile[:, None])
    shares = jnp.zeros((count, 1, BLOCK), F32)
    remapped, heating, shares = heat(inside, rows - 2, bounds, e, rows, lambda r: r + 1, *other, shares)
    made = (remapped, heating)
    remapped, heating, shares = heat(outside, 2, bounds, e, rows, lambda r: r * (rows - 1), *other, shares, made)
    later = lambda r: r + EARLY * jnp.minimum(r, 1)
    remapped = remap(second, 0, rows - EARLY, later, bounds, e, remapped)
    owner_heat = jnp.sum(lax.all_to_all(shares, "lat", split_axis=0, concat_axis=0, tiled=True)).reshape(1, 1)
    return (remapped, heating, owner_heat)


def solution(mesh):
    placed = (
        P(None, "lat", "lev", None),
        P("lat", "lev", None),
        P("lat", "lev", None),
        P("lat", "lev", None),
        P(),
        P(),
        P(("lat", "lev"), None),
        P(("lat", "lev")),
    )
    return jax.shard_map(
        per_device,
        mesh=mesh,
        in_specs=placed,
        out_specs=(P(None, "lat", None, "lev"), P("lat", None, "lev"), P("lat", "lev")),
        check_vma=False,
    )
```
